32 devices in a mesh: groups: 2 (over y), occ: 4 (over z), vir: 4 (over x, core).
Axes of the slice: x: 2, y: 2, z: 4, core: 2. Of those that a mesh axis runs over, the one named last changes fastest.
Arguments:
- amplitudes: bfloat16 [32, 400, 24, 128], P(('groups', 'occ'), None, 'vir'), parts along dimension 0, may hold values from -6 to 6
- amp_keep: int32 [32, 24], P(('groups', 'occ'), 'vir'), parts along dimension 0, may hold values 0 or 1
- integrals: bfloat16 [48, 128, 24, 128], P(('groups', 'vir')), parts along dimension 0, may hold values from -0.3125 to 0.3125
- int_keep: int32 [48, 24], P(('groups', 'vir')), parts along dimension 0, may hold values 0 or 1
- fock_vir: bfloat16 [48, 128, 128], P(('groups', 'vir')), parts along dimension 0, may hold values from -0.5 to 0.5
- fock_occ: bfloat16 [32, 400, 400], P(('groups', 'occ')), parts along dimension 0, may hold values from -0.3125 to 0.3125
- occ_energy: float32 [32, 400], P(('groups', 'occ')), parts along dimension 0, may hold values from -2 to -0.4
- vir_energy: float32 [48, 128], P(('groups', 'vir')), parts along dimension 0, may hold values from 0.4 to 3
- res_keep: int32 [32, 24], P(('groups', 'occ'), 'vir'), parts along dimension 0, may hold values 0 or 1
- res_place: int32 [32, 24], P(('groups', 'occ'), 'vir'), parts along dimension 0, may hold values from 0 to 95, as said below
Outputs:
- residual_tiles: float32 [192, 4, 400, 128], P(('groups', 'occ'), 'vir'), parts along dimension 0
- new_amplitudes: float32 [192, 4, 400, 128], P(('groups', 'occ'), 'vir'), parts along dimension 0
The draws below stay inside these ranges and needn't reach their ends.
There are 2 independent parts, one for each index of `groups`. The reference program is written for one: setup_inputs(seed, part) draws one part's arguments, and reference() takes and returns one part's arrays. A program takes and returns all parts, laid end to end along the dimension named above; each array names one. Nothing has to cross between parts.
Inputs may be any that keep to these rules, and one draw needn't show every extreme that they name: Within each run of 6 virtual tiles, res_place maps the tiles of all pair tiles one to one onto 0 to 95. The tiles of one aligned run of 4 pair tiles within one such virtual run reach at most 6 values in any aligned run of 24 values, and exactly 6 in some.
All inputs are finite; a program needn't handle non-finite values. No bound on the sum of `amp_keep` or of `int_keep` or of `res_keep` on one device may be relied on, other than what follows from the above.
Results may differ from the reference program's by a relative error of at most 0.0003.
Values may be sent and summed in bfloat16 or wider, within the bound.
No kernel may reach another device: no remote copies, remote signals or barrier semaphores. Data moves between devices by JAX's collectives and lax.ppermute only.
A program may use at most 128 MiB of HBM per device.

```python
import jax
import jax.numpy as jnp
from jax import lax

VT = 128
NVT = 24
P_DEV = 4
ROWS = 400
NP = 16
CPV = 6
TD = 24
CAP = 6
N_VIR = 4


def draw_res_place(key, part):
    key = jax.random.fold_in(key, 7)
    sources = NP // P_DEV
    column_count = NVT // CPV
    offset_count = (TD + CAP - 1) // CAP
    pieces = []
    for column in range(column_count):
        key_off, key_src, key_dst = jax.random.split(jax.random.fold_in(key, column), 3)
        offsets = jax.random.permutation(key_off, sources)[:offset_count].astype(jnp.int32)
        src_perm = jax.vmap(lambda sub: jax.random.permutation(sub, TD))(jax.random.split(key_src, sources)).astype(jnp.int32)
        dst_perm = jax.vmap(lambda sub: jax.random.permutation(sub, TD))(jax.random.split(key_dst, sources)).astype(jnp.int32)
        target = (jnp.arange(sources, dtype=jnp.int32)[:, None] + offsets[src_perm // CAP]) % sources
        slots = target * TD + dst_perm[target, src_perm]
        arranged = jnp.transpose(slots.reshape(sources, CPV, P_DEV), (0, 2, 1)).reshape(NP, CPV)
        pieces.append(arranged)
    return jnp.concatenate(pieces, axis=1).astype(jnp.int32)


def plant(entries, stream_key, least, top_value):
    extent = entries.shape
    index_at = [jax.random.randint(jax.random.fold_in(stream_key, axis), (), 0, extent[axis]) for axis in range(len(extent))]
    entries = entries.at[tuple(index_at)].set(least)
    longest = extent.index(max(extent))
    index_at[longest] = (index_at[longest] + 1) % extent[longest]
    return entries.at[tuple(index_at)].set(top_value)


def levels(key, extent, shards, low, largest):
    loudness = 1.0
    for position, blocks in shards:
        heights = jax.random.uniform(jax.random.fold_in(jax.random.fold_in(key, 6), position), (blocks,), jnp.float32, low / len(shards), largest / len(shards))
        loudness = loudness * jnp.repeat(jnp.exp(heights), extent[position] // blocks).reshape((-1,) + (1,) * (len(extent) - 1 - position))
    return loudness


def scatter_about(own_key, extent, deviation, limit, shards=(), held_as=jnp.bfloat16):
    drawn = deviation * jax.random.normal(own_key, extent, jnp.float32)
    if shards:
        drawn = drawn * levels(own_key, extent, shards, -0.22, 0.18)
    return jnp.clip(drawn, -limit, limit).astype(held_as)


def setup_inputs(seed: int = 0, part: int = 0) -> dict:
    seeds = jax.random.split(jax.random.key(seed), 11)
    own_keys = jax.random.split(jax.random.fold_in(seeds[10], part), 11)
    amplitudes = scatter_about(own_keys[0], (NP, ROWS, NVT, VT), 1.0, 6.0, ((0, 4), (2, 4)))
    amp_keep = plant((jax.random.randint(own_keys[1], (NP, NVT), 0, 3) < 1).astype(jnp.int32), jax.random.fold_in(own_keys[1], 1), 0, 1)
    integrals = scatter_about(own_keys[2], (NVT, VT, NVT, VT), (NVT * VT // 9) ** -0.5, 0.3125, ((0, 4),))
    int_keep = plant((jax.random.randint(own_keys[3], (NVT, NVT), 0, 3) < 1).astype(jnp.int32), jax.random.fold_in(own_keys[3], 1), 0, 1)
    fock_vir = scatter_about(own_keys[4], (NVT, VT, VT), VT ** -0.5, 0.5, ((0, 4),))
    fock_occ = scatter_about(own_keys[5], (NP, ROWS, ROWS), ROWS ** -0.5, 0.3125, ((0, 4),))
    occ_energy = jnp.clip(-2.0 + 1.6 * jax.random.uniform(own_keys[6], (NP, ROWS), jnp.float32) ** levels(own_keys[6], (NP, ROWS), ((0, 4),), -0.2, 0.2), -2.0, -0.4)
    vir_energy = jnp.clip(0.4 + 2.6 * jax.random.uniform(own_keys[7], (NVT, VT), jnp.float32) ** levels(own_keys[7], (NVT, VT), ((0, 4),), -0.2, 0.2), 0.4, 3.0)
    res_keep = plant((jax.random.randint(own_keys[8], (NP, NVT), 0, 2) < 1).astype(jnp.int32), jax.random.fold_in(own_keys[8], 1), 0, 1)
    res_place = draw_res_place(jax.random.fold_in(jax.random.fold_in(seeds[10], part), 71), part)
    return {"amplitudes": amplitudes, "amp_keep": amp_keep, "integrals": integrals, "int_keep": int_keep, "fock_vir": fock_vir, "fock_occ": fock_occ, "occ_energy": occ_energy, "vir_energy": vir_energy, "res_keep": res_keep, "res_place": res_place}


def reference(amplitudes, amp_keep, integrals, int_keep, fock_vir, fock_occ, occ_energy, vir_energy, res_keep, res_place):
    kept_amps = amplitudes * amp_keep[:, None, :, None].astype(jnp.bfloat16)
    masked_ints = integrals * int_keep[:, None, :, None].astype(jnp.bfloat16)
    matrix = masked_ints.reshape(NVT * VT, NVT * VT)
    fock_wide = fock_vir.astype(jnp.float32)

    def one_pair(index):
        tile = kept_amps[index]
        ladder = jnp.dot(tile.reshape(ROWS, NVT * VT), matrix, preferred_element_type=jnp.float32).reshape(ROWS, NVT, VT)
        wide = tile.astype(jnp.float32)
        vir_term = jnp.einsum("rAc,Aca->rAa", wide, fock_wide)
        occ_term = jnp.einsum("rs,sAa->rAa", fock_occ[index].astype(jnp.float32), wide)
        keep_mask = res_keep[index].astype(jnp.float32)[None, :, None]
        resid = keep_mask * (ladder + vir_term - occ_term)
        denominator = vir_energy[None, :, :] - occ_energy[index][:, None, None]
        return resid, wide + resid / denominator

    resid, update = lax.map(one_pair, jnp.arange(NP).astype(jnp.int32))
    columns = jnp.broadcast_to((jnp.arange(NVT).astype(jnp.int32) // CPV)[None, :], (NP, NVT))
    empty = jnp.zeros((NP * CPV, N_VIR, ROWS, VT), jnp.float32)
    residual_tiles = empty.at[res_place, columns].set(jnp.transpose(resid, (0, 2, 1, 3)))
    new_amplitudes = empty.at[res_place, columns].set(jnp.transpose(update, (0, 2, 1, 3)))
    return residual_tiles, new_amplitudes
```

```python
import functools

import jax
import jax.numpy as jnp
from jax import lax
from jax.experimental import pallas as pl
from jax.experimental.pallas import tpu as pltpu
from jax.sharding import PartitionSpec as P

CODE_ROWS = 16
LEVELS = 32700.0
VMEM_BYTES = 48 * 1024 * 1024
ANY = pl.BlockSpec(memory_space=pl.ANY)


def params():
    return pltpu.CompilerParams(vmem_limit_bytes=VMEM_BYTES)


def held(array):
    rank = len(array.shape)
    return pl.BlockSpec(array.shape, lambda i, table: (0,) * rank, pipeline_mode=pl.Buffered(1))


def scale_block(rows):
    return 80 if rows % 80 == 0 else rows


def encode(values, out_ref):
    rows, width = values.shape
    block = scale_block(rows)
    cut = values.reshape(rows // block, block, width)
    top = jnp.max(jnp.abs(cut), axis=1, keepdims=True)
    step = jnp.clip(jnp.ceil(8.0 * jnp.log2(jnp.maximum(top, 1e-30))), -800.0, 800.0)
    whole = jnp.round(cut * (LEVELS * jnp.exp2(step * -0.125))).reshape(rows, width)
    out_ref[0, :rows, :] = whole.astype(jnp.int32).astype(jnp.int16)
    steps = step.reshape(rows // block, width)
    steps = jnp.concatenate([steps, jnp.zeros((CODE_ROWS - rows // block, width), jnp.float32)], axis=0)
    out_ref[0, rows:, :] = steps.astype(jnp.int32).astype(jnp.int16)


def decode(coded):
    rows, width = coded.shape[0] - CODE_ROWS, coded.shape[1]
    block = scale_block(rows)
    steps = coded[rows:, :].astype(jnp.int32).astype(jnp.float32)[: rows // block]
    scale = jnp.exp2(steps * 0.125) * (1.0 / LEVELS)
    whole = coded[:rows, :].astype(jnp.int32).astype(jnp.float32)
    return (whole.reshape(rows // block, block, width) * scale.reshape(rows // block, 1, width)).reshape(rows, width)


def add_ladder(total, table, base, tile, blocks, runs, run, amps_own, amps_other, ints_own, ints_other):
    pair, column = tile // blocks, tile % blocks
    tiles = amps_own.shape[0]
    ints_len = blocks * runs * blocks
    for part, (amps, ints) in enumerate(((amps_own, ints_own), (amps_other, ints_other))):
        amp_base = base + part * tiles
        int_base = base + 2 * tiles + part * ints_len

        def step(block, carry):
            source = pair * blocks + block
            kept = table[amp_base + source] * table[int_base + (block * runs + run) * blocks + column]

            @pl.when(kept != 0)
            def _():
                total[...] += jnp.dot(amps[source], ints[run, column, block], preferred_element_type=jnp.float32)

            return carry

        lax.fori_loop(0, blocks, step, 0)


def sums_kernel(blocks, runs, per_chunk, chunks, table, amps_own, amps_other, ints_own, ints_other, *refs):
    outs, total = refs[:chunks], refs[chunks]
    entries = per_chunk * chunks
    i = pl.program_id(0)
    tile = table[i]

    @pl.when(tile >= 0)
    def _():
        total[...] = jnp.zeros_like(total)
        run = table[entries]
        add_ladder(total, table, entries + 1, tile, blocks, runs, run, amps_own, amps_other, ints_own, ints_other)
        for chunk in range(chunks):

            @pl.when(i // per_chunk == chunk)
            def _():
                encode(total[...], outs[chunk])


def own_kernel(
    blocks, runs, entries, table, amps_own, amps_other, ints_own, ints_other, fock_vir, fock_occ, out, total
):
    tile = table[pl.program_id(0)]

    @pl.when(tile >= 0)
    def _():
        total[...] = jnp.zeros_like(total)
        run = table[entries]
        add_ladder(total, table, entries + 1, tile, blocks, runs, run, amps_own, amps_other, ints_own, ints_other)

        @pl.when(table[entries + 1 + tile] != 0)
        def _():
            amps = amps_own[tile]
            total[...] += jnp.dot(amps, fock_vir[tile % blocks], preferred_element_type=jnp.float32)
            total[...] -= jnp.dot(fock_occ[tile // blocks], amps, preferred_element_type=jnp.float32)

        out[0] = total[...]


def join_kernel(others, per_dest, dests, first, table, own, *refs):
    came, outs = refs[:others], refs[others:]
    i = pl.program_id(0)

    @pl.when(table[first + i] >= 0)
    def _():
        total = own[0]
        for ref in came:
            total = total + decode(ref[0])
        for dest in range(dests):

            @pl.when(i // per_dest == dest)
            def _():
                encode(total, outs[dest])


def pack_kernel(dests, slots, table, amps, *refs):
    outs, sem = refs[:dests], refs[dests]
    copies = [
        pltpu.make_async_copy(amps.at[table[dest * slots + slot]], outs[dest].at[slot], sem.at[dest * slots + slot])
        for dest in range(dests)
        for slot in range(slots)
    ]
    for copy in copies:
        copy.start()
    for copy in copies:
        copy.wait()


def final_kernel(chunks, dests, per_dest, table, occ_cols, vir_energy, *refs):
    codes = refs[: chunks * dests]
    amps = refs[chunks * dests : chunks * dests + dests]
    out_res, out_upd, held_codes, held_amps, sem = refs[chunks * dests + dests :]
    slot = pl.program_id(0)
    slots_all = pl.num_programs(0)

    @pl.when(slot == 0)
    def _():
        copies = []
        for n, ref in enumerate(codes):
            copies.append(
                pltpu.make_async_copy(ref, held_codes.at[pl.ds(n * per_dest, per_dest)], sem.at[n])
            )
        many = chunks * per_dest
        for n, ref in enumerate(amps):
            copies.append(
                pltpu.make_async_copy(ref, held_amps.at[pl.ds(n * many, many)], sem.at[len(codes) + n])
            )
        for copy in copies:
            copy.start()
        for copy in copies:
            copy.wait()

    def entry(row):
        return table[row * slots_all + slot]

    rows, width = out_res.shape[2], out_res.shape[3]
    res_kept, amp_kept = entry(4) != 0, entry(5) != 0
    resid = jnp.where(res_kept, decode(held_codes[entry(0)]), 0.0)
    kept = jnp.where(amp_kept, held_amps[entry(1)].astype(jnp.float32), 0.0)
    lane = lax.broadcasted_iota(jnp.int32, (rows, width), 1)
    occ = jnp.sum(jnp.where(lane == entry(2), occ_cols[...], 0.0), axis=1, keepdims=True)
    vir = vir_energy[pl.ds(entry(3), 1), :]
    out_res[0, 0] = resid
    out_upd[0, 0] = kept + resid / (vir - occ)


def body(
    amplitudes,
    amp_keep,
    integrals,
    int_keep,
    fock_vir,
    fock_occ,
    occ_energy,
    vir_energy,
    res_keep,
    res_place,
):
    pairs, rows, blocks, width = amplitudes.shape
    dests, virs = lax.axis_size("occ"), lax.axis_size("vir")
    runs = virs // 2
    me_occ, me_vir = lax.axis_index("occ"), lax.axis_index("vir")
    core, chip = me_vir % 2, me_vir // 2
    tiles = pairs * blocks
    slots = max(2, (tiles + dests - 1) // dests)
    chunks = 3 if slots % 3 == 0 else slots
    per_dest = slots // chunks
    per_chunk = per_dest * dests
    entries = chunks * per_chunk
    coded_rows = rows + CODE_ROWS

    def swap(array, axis, bit):
        size = lax.axis_size(axis)
        return lax.ppermute(array, axis, [(i, i ^ bit) for i in range(size)])

    places = res_place.reshape(tiles)
    res_kept = res_keep.reshape(tiles)
    amp_kept = amp_keep.reshape(tiles)
    toward = (places // tiles) ^ me_occ
    order = jnp.arange(tiles, dtype=jnp.int32)
    key = order + jnp.where(res_kept != 0, 0, tiles)
    earlier = (toward[None, :] == toward[:, None]) & (key[None, :] < key[:, None])
    rank = jnp.sum(earlier.astype(jnp.int32), axis=1)
    match = (toward[None, None, :] == jnp.arange(dests, dtype=jnp.int32)[:, None, None]) & (
        rank[None, None, :] == jnp.arange(slots, dtype=jnp.int32)[None, :, None]
    )
    fields = jnp.stack([places % tiles + 1, order, res_kept, amp_kept])
    meta = jnp.sum(jnp.where(match[None], fields[:, None, None, :], 0), axis=3)
    slot_tile = meta[1]
    todo = jnp.where((meta[0] > 0) & (meta[2] != 0), slot_tile, -1)
    todo = jnp.transpose(todo.reshape(dests, chunks, per_dest), (1, 0, 2)).reshape(entries)
    todo_other = [swap(todo, "vir", 2 * k) for k in range(1, runs)]

    amps = jnp.transpose(amplitudes, (0, 2, 1, 3)).reshape(tiles, rows, width)

    packed = pl.pallas_call(
        functools.partial(pack_kernel, dests, slots),
        out_shape=[jax.ShapeDtypeStruct((slots, rows, width), amps.dtype)] * dests,
        grid_spec=pltpu.PrefetchScalarGridSpec(
            num_scalar_prefetch=1,
            grid=(1,),
            in_specs=[ANY],
            out_specs=[ANY] * dests,
            scratch_shapes=[pltpu.SemaphoreType.DMA((dests * slots,))],
        ),
        compiler_params=params(),
        cost_estimate=pl.CostEstimate(flops=0, bytes_accessed=4 * amps.size, transcendentals=0),
        name="pack_amps",
    )(slot_tile.reshape(dests * slots), amps)
    amps_came = [packed[0]] + [swap(packed[s], "occ", s) for s in range(1, dests)]

    by_core = jnp.transpose(integrals.reshape(blocks, width, runs, 2, blocks, width), (3, 2, 4, 0, 1, 5))
    ints_own = lax.dynamic_index_in_dim(by_core, core, 0, keepdims=False)
    ints_other = swap(lax.dynamic_index_in_dim(by_core, 1 - core, 0, keepdims=False), "vir", 1)
    amps_other = swap(amps, "vir", 1)
    keep_by_core = jnp.transpose(int_keep.reshape(blocks, runs, 2, blocks), (2, 0, 1, 3)).reshape(2, -1)
    keep_own = lax.dynamic_index_in_dim(keep_by_core, core, 0, keepdims=False)
    keep_send = lax.dynamic_index_in_dim(keep_by_core, 1 - core, 0, keepdims=False)
    keep_came = swap(jnp.concatenate([amp_kept, keep_send]), "vir", 1)
    keeps = jnp.concatenate([amp_kept, keep_came[:tiles], keep_own, keep_came[tiles:]])

    shared = (amps, amps_other, ints_own, ints_other)
    share_specs = [held(a) for a in shared]
    flops = 2 * tiles * rows * width * width
    tile_bytes = rows * width

    def clamped(first, count):
        return lambda i, table: (jnp.clip(i - first, 0, count - 1), 0, 0)

    sums_came = []
    for k in range(1, runs):
        sums = pl.pallas_call(
            functools.partial(sums_kernel, blocks, runs, per_chunk, chunks),
            out_shape=[jax.ShapeDtypeStruct((per_chunk, coded_rows, width), jnp.int16)] * chunks,
            grid_spec=pltpu.PrefetchScalarGridSpec(
                num_scalar_prefetch=1,
                grid=(entries,),
                in_specs=share_specs,
                out_specs=[
                    pl.BlockSpec((1, coded_rows, width), clamped(c * per_chunk, per_chunk)) for c in range(chunks)
                ],
                scratch_shapes=[pltpu.VMEM((rows, width), jnp.float32)],
            ),
            compiler_params=params(),
            cost_estimate=pl.CostEstimate(flops=4 * flops, bytes_accessed=8 * tiles * tile_bytes, transcendentals=0),
            name="ladder_sums",
        )(jnp.concatenate([todo_other[k - 1], (chip ^ k)[None], keeps]), *shared)
        sums_came.append([swap(sums[c], "vir", 2 * k) for c in range(chunks)])

    own = pl.pallas_call(
        functools.partial(own_kernel, blocks, runs, entries),
        out_shape=jax.ShapeDtypeStruct((entries, rows, width), jnp.float32),
        grid_spec=pltpu.PrefetchScalarGridSpec(
            num_scalar_prefetch=1,
            grid=(entries,),
            in_specs=share_specs + [held(fock_vir), held(fock_occ)],
            out_specs=pl.BlockSpec((1, rows, width), lambda i, table: (i, 0, 0)),
            scratch_shapes=[pltpu.VMEM((rows, width), jnp.float32)],
        ),
        compiler_params=params(),
        cost_estimate=pl.CostEstimate(flops=4 * flops, bytes_accessed=10 * tiles * tile_bytes, transcendentals=0),
        name="own_part",
    )(jnp.concatenate([todo, chip[None], keeps]), *shared, fock_vir, fock_occ)

    codes = []
    for c in range(chunks):
        first = c * per_chunk
        joined = pl.pallas_call(
            functools.partial(join_kernel, runs - 1, per_dest, dests, first),
            out_shape=[jax.ShapeDtypeStruct((per_dest, coded_rows, width), jnp.int16)] * dests,
            grid_spec=pltpu.PrefetchScalarGridSpec(
                num_scalar_prefetch=1,
                grid=(per_chunk,),
                in_specs=[pl.BlockSpec((1, rows, width), lambda i, table, first=first: (first + i, 0, 0))]
                + [pl.BlockSpec((1, coded_rows, width), lambda i, table: (i, 0, 0))] * (runs - 1),
                out_specs=[pl.BlockSpec((1, coded_rows, width), clamped(s * per_dest, per_dest)) for s in range(dests)],
            ),
            compiler_params=params(),
            cost_estimate=pl.CostEstimate(
                flops=10 * per_chunk * tile_bytes, bytes_accessed=8 * per_chunk * tile_bytes, transcendentals=0
            ),
            name="join_parts",
        )(todo, own, *[came[c] for came in sums_came])
        codes += [joined[0]] + [swap(joined[s], "occ", s) for s in range(1, dests)]

    notes = [jnp.concatenate([occ_energy.reshape(-1), meta[:, s].reshape(-1).astype(jnp.float32)]) for s in range(dests)]
    notes = jnp.stack([notes[0]] + [swap(notes[s], "occ", s) for s in range(1, dests)])
    occ_all = notes[:, : pairs * rows].reshape(dests * pairs, rows)
    occ_cols = jnp.transpose(jnp.pad(occ_all, ((0, width - dests * pairs), (0, 0))))
    info = notes[:, pairs * rows :].astype(jnp.int32).reshape(dests, 4, slots)
    source = jnp.arange(dests, dtype=jnp.int32)[:, None]
    place = jnp.arange(slots, dtype=jnp.int32)[None, :]
    code_at = (place // per_dest) * per_chunk + source * per_dest + place % per_dest
    amps_at = source * slots + place
    columns = jnp.stack([code_at, amps_at, source * pairs + info[:, 1] // blocks, info[:, 1] % blocks, info[:, 2], info[:, 3]])
    here = info[:, 0][None] == jnp.arange(1, tiles + 1, dtype=jnp.int32)[:, None, None]
    table = jnp.sum(jnp.where(here[None], columns[:, None], 0), axis=(2, 3)).reshape(-1)

    return pl.pallas_call(
        functools.partial(final_kernel, chunks, dests, per_dest),
        out_shape=[jax.ShapeDtypeStruct((tiles, 1, rows, width), jnp.float32)] * 2,
        grid_spec=pltpu.PrefetchScalarGridSpec(
            num_scalar_prefetch=1,
            grid=(tiles,),
            in_specs=[held(occ_cols), held(vir_energy)] + [ANY] * (chunks * dests + dests),
            out_specs=[pl.BlockSpec((1, 1, rows, width), lambda i, table: (i, 0, 0, 0))] * 2,
            scratch_shapes=[
                pltpu.VMEM((entries, coded_rows, width), jnp.int16),
                pltpu.VMEM((entries, rows, width), jnp.bfloat16),
                pltpu.SemaphoreType.DMA((chunks * dests + dests,)),
            ],
        ),
        compiler_params=params(),
        cost_estimate=pl.CostEstimate(
            flops=10 * tiles * tile_bytes, bytes_accessed=12 * tiles * tile_bytes, transcendentals=0
        ),
        name="update_tiles",
    )(table, occ_cols, vir_energy, *codes, *amps_came)


def solution(mesh):
    return jax.shard_map(
        body,
        mesh=mesh,
        in_specs=(
            P(("groups", "occ"), None, "vir", None),
            P(("groups", "occ"), "vir"),
            P(("groups", "vir"), None, None, None),
            P(("groups", "vir"), None),
            P(("groups", "vir"), None, None),
            P(("groups", "occ"), None, None),
            P(("groups", "occ"), None),
            P(("groups", "vir"), None),
            P(("groups", "occ"), "vir"),
            P(("groups", "occ"), "vir"),
        ),
        out_specs=(
            P(("groups", "occ"), "vir", None, None),
            P(("groups", "occ"), "vir", None, None),
        ),
        check_vma=False,
    )
```

```python
import collections
import functools

import jax
import jax.numpy as jnp
from jax import lax
from jax.experimental import pallas as pl
from jax.experimental.pallas import tpu as pltpu
from jax.sharding import PartitionSpec as P

CODE_ROWS = 16
LEVELS = 32700.0
MIB = 1024 * 1024
AMPS = 1024
FIELDS = 4
NOTE_ROWS = 16
PARTS = 3
HBM = pl.BlockSpec(memory_space=pltpu.HBM)
SMEM = pl.BlockSpec(memory_space=pltpu.SMEM)
VMEM = pl.BlockSpec(memory_space=pltpu.VMEM)
SIZE_NAMES = ("pairs", "rows", "blocks", "width", "dests", "runs", "tiles", "slots", "early", "extra")
SIZE_NAMES += ("starts", "entries")
Size = collections.namedtuple("Size", SIZE_NAMES)


def call(kernel, name, inputs, in_specs, out_shape, out_specs, scratch, vmem, aliases=None):
    return pl.pallas_call(
        kernel,
        out_shape=out_shape,
        in_specs=in_specs,
        out_specs=out_specs,
        scratch_shapes=scratch,
        input_output_aliases=aliases or {},
        compiler_params=pltpu.CompilerParams(vmem_limit_bytes=vmem * MIB),
        name=name,
    )(*inputs)


def chunk_of(size, slot):
    return sum((slot >= start).astype(jnp.int32) for start in size.starts[1:-1])


def scale_block(rows):
    return 80 if rows % 80 == 0 else rows


def encode(values, out):
    rows, width = values.shape
    block = scale_block(rows)
    cut = values.reshape(rows // block, block, width)
    top = jnp.max(jnp.abs(cut), axis=1, keepdims=True)
    step = jnp.clip(jnp.ceil(8.0 * jnp.log2(jnp.maximum(top, 1e-30))), -800.0, 800.0)
    whole = jnp.round(cut * (LEVELS * jnp.exp2(step * -0.125))).reshape(rows, width)
    out[:rows, :] = whole.astype(jnp.int32).astype(jnp.int16)
    steps = step.reshape(rows // block, width)
    steps = jnp.concatenate([steps, jnp.zeros((CODE_ROWS - rows // block, width), jnp.float32)], axis=0)
    out[rows:, :] = steps.astype(jnp.int32).astype(jnp.int16)


def decode(coded):
    rows, width = coded.shape[0] - CODE_ROWS, coded.shape[1]
    block = scale_block(rows)
    steps = coded[rows:, :].astype(jnp.int32).astype(jnp.float32)[: rows // block]
    scale = jnp.exp2(steps * 0.125) * (1.0 / LEVELS)
    whole = coded[:rows, :].astype(jnp.int32).astype(jnp.float32)
    return (whole.reshape(rows // block, block, width) * scale.reshape(rows // block, 1, width)).reshape(rows, width)


def plan_kernel(size, place_in, res_keep_in, amp_keep_in, int_keep_in, occ_energy, amps, *refs):
    late, spots, wanted, extra, mask_own, mask_send, packed = refs[:7]
    place, res_keep, amp_keep, int_keep, word_sem = refs[7:12]
    notes, early_at, res_count, amp_count, all_count, res_seen, stage, energies, note, come_sem, go_sem, note_sem = refs[12:]
    words_in = [
        pltpu.make_async_copy(source, target, word_sem.at[n])
        for n, (source, target) in enumerate(
            ((place_in, place), (res_keep_in, res_keep), (amp_keep_in, amp_keep), (int_keep_in, int_keep))
        )
    ]
    for copy in words_in:
        copy.start()
    me, core = lax.axis_index("occ"), lax.rem(lax.axis_index("vir"), 2)

    for s in range(size.dests):
        for ref in (res_count, amp_count, all_count, res_seen):
            ref[s] = 0
    for ref, count, value in (
        (late, size.entries, -1),
        (spots, size.entries, 0),
        (wanted, size.tiles, -1),
        (extra, size.dests * size.extra, -1),
        (early_at, size.dests * size.early, -1),
        (notes, size.dests * size.slots * FIELDS, 0),
    ):

        def clear(n, carry, ref=ref, value=value):
            ref[n] = value
            return carry

        lax.fori_loop(0, count, clear, 0)

    for copy in words_in:
        copy.wait()

    res_seen[size.dests] = 0

    def entry(s, slot):
        at = s * size.starts[1] + slot
        for low, high in zip(size.starts[1:-1], size.starts[2:]):
            at = jnp.where(slot >= low, low * size.dests + s * (high - low) + slot - low, at)
        return at

    def residuals(tile, carry):
        pair, column = tile // size.blocks, lax.rem(tile, size.blocks)
        s = (place[pair, column] // size.tiles) ^ me

        @pl.when(res_keep[pair, column] != 0)
        def _():
            slot = res_count[s]
            res_count[s] = slot + 1
            late[entry(s, slot)] = tile

        return carry

    lax.fori_loop(0, size.tiles, residuals, 0)

    def amplitudes(tile, carry):
        pair, column = tile // size.blocks, lax.rem(tile, size.blocks)
        where = place[pair, column]
        target = where // size.tiles
        s = target ^ me
        first = (s * size.slots + all_count[s]) * FIELDS
        all_count[s] = all_count[s] + 1
        notes[first] = where - target * size.tiles + 1
        notes[first + 1] = tile
        notes[first + 2] = -1
        notes[first + 3] = -1

        @pl.when(res_keep[pair, column] != 0)
        def _():
            notes[first + 2] = res_seen[s]
            res_seen[s] = res_seen[s] + 1

        @pl.when(amp_keep[pair, column] != 0)
        def _():
            rank = amp_count[s]
            amp_count[s] = rank + 1
            slot = size.slots - 1 - (rank - size.early)

            @pl.when(rank < size.early)
            def _():
                n = s * size.early + rank
                early_at[n] = tile
                notes[first + 3] = rank
                pltpu.make_async_copy(amps.at[tile], stage.at[n], come_sem.at[n]).start()

            @pl.when((rank >= size.early) & (slot >= res_count[s]))
            def _():
                late[entry(s, slot)] = tile + AMPS
                notes[first + 3] = size.early + slot

            @pl.when((rank >= size.early) & (slot < res_count[s]))
            def _():
                extra[s * size.extra + rank - size.early] = tile
                notes[first + 3] = size.slots + rank
                res_seen[size.dests] = 1

        return carry

    lax.fori_loop(0, size.tiles, amplitudes, 0)

    for s in range(size.dests):
        for slot in range(size.early):
            n = s * size.early + slot

            @pl.when(early_at[n] >= 0)
            def _(s=s, slot=slot, n=n):
                rows = pl.ds(slot * size.rows, size.rows)
                pltpu.make_async_copy(amps.at[0], stage.at[n], come_sem.at[n]).wait()
                pltpu.make_async_copy(stage.at[n], packed.at[me ^ s, rows], go_sem.at[n]).start()

    energies[...] = jnp.zeros((NOTE_ROWS, size.width), jnp.float32)
    strips = -(-size.rows // size.width)
    for pair in range(size.pairs):
        for strip in range(strips):
            low, high = strip * size.width, min(size.rows, (strip + 1) * size.width)
            energies[pair * strips + strip : pair * strips + strip + 1, : high - low] = occ_energy[pair : pair + 1, low:high]
    left = energies[...]
    lane = lax.broadcasted_iota(jnp.int32, (NOTE_ROWS, size.width), 1)
    parts = []
    for _ in range(PARTS):
        parts.append(left.astype(jnp.bfloat16))
        left = left - parts[-1].astype(jnp.float32)
    for s in range(size.dests):
        for n, part in enumerate(parts):
            note[s, n * NOTE_ROWS : (n + 1) * NOTE_ROWS] = part
        words = jnp.where(lane == size.slots * FIELDS, res_seen[size.dests], 0)
        for n in range(size.slots * FIELDS):
            words = jnp.where(lane == n, notes[s * size.slots * FIELDS + n], words)
        note[s, PARTS * NOTE_ROWS :] = words.astype(jnp.float32).astype(jnp.bfloat16)
        target = packed.at[me ^ s, pl.ds(size.early * size.rows, (PARTS + 1) * NOTE_ROWS)]
        pltpu.make_async_copy(note.at[s], target, note_sem.at[s]).start()

    def compact(n, count):
        what = late[n]
        kept = (what >= 0) & (what < AMPS)

        @pl.when(kept)
        def _():
            wanted[count] = what
            spots[n] = count

        return count + kept.astype(jnp.int32)

    lax.fori_loop(0, size.entries, compact, jnp.int32(0))

    for pair in range(size.pairs):
        mask = amp_keep[pair, 0]
        for block in range(1, size.blocks):
            mask = mask | (amp_keep[pair, block] << block)
        mask_own[pair] = mask
        mask_send[pair] = mask

    def integrals(n, carry):
        run, column = n // size.blocks, lax.rem(n, size.blocks)
        for target, parity in ((mask_own, core), (mask_send, 1 - core)):
            at = (run * 2 + parity) * size.blocks + column
            mask = int_keep[0, at]
            for block in range(1, size.blocks):
                mask = mask | (int_keep[block, at] << block)
            target[size.pairs + n] = mask
        return carry

    lax.fori_loop(0, size.runs * size.blocks, integrals, 0)

    for s in range(size.dests):
        for slot in range(size.early):
            n = s * size.early + slot

            @pl.when(early_at[n] >= 0)
            def _(s=s, slot=slot, n=n):
                pltpu.make_async_copy(stage.at[n], packed.at[0, pl.ds(0, size.rows)], go_sem.at[n]).wait()

        target = packed.at[0, pl.ds(0, (PARTS + 1) * NOTE_ROWS)]
        pltpu.make_async_copy(note.at[s], target, note_sem.at[s]).wait()


def integral_tile(ints, block, place, wide):
    for first in range(0, ints.shape[2], 8):

        @pl.when((place >= first) & (place < first + 8))
        def _(first=first):
            part = ints[block, :, first : first + 8, :].astype(jnp.float32)
            wide[...] = part.reshape(wide.shape)

    return wide[pl.ds(lax.rem(place, 8), ints.shape[1], stride=8), :].astype(ints.dtype)


def add_ladder(size, total, tile, run, mask, amps, ints, wide):
    pair, column = tile // size.blocks, lax.rem(tile, size.blocks)
    place = (run * 2 + lax.rem(lax.axis_index("vir"), 2)) * size.blocks + column
    active = mask[pair] & mask[size.pairs + run * size.blocks + column]
    for block in range(size.blocks):

        @pl.when(((active >> block) & 1) != 0)
        def _(block=block):
            total[...] += jnp.dot(
                amps[pair * size.blocks + block],
                integral_tile(ints, block, place, wide),
                preferred_element_type=jnp.float32,
            )


def two_parts(size, wanted, run, mask_own, mask_other, own, others, copies, totals, wide, more, last):
    for copy in copies:
        copy.start()

    def mine(n, carry):
        tile = wanted[n]

        @pl.when(tile >= 0)
        def _():
            total = totals.at[n]
            total[...] = jnp.zeros((size.rows, size.width), jnp.float32)
            add_ladder(size, total, tile, run, mask_own, *own, wide)
            more(tile, total)

        return carry

    def theirs(n, carry):
        tile = wanted[n]

        @pl.when(tile >= 0)
        def _():
            add_ladder(size, totals.at[n], tile, run, mask_other, *others, wide)
            last(n, totals.at[n])

        return carry

    lax.fori_loop(0, size.tiles, mine, 0)
    for copy in copies:
        copy.wait()
    lax.fori_loop(0, size.tiles, theirs, 0)


def sums_kernel(size, pieces, step, wanted, mask_own, mask_other, amps_own, ints_own, amps_other, ints_other, *refs):
    outs, refs = refs[: len(pieces)], refs[len(pieces) :]
    totals, stage, amps_here, ints_here, wide, come_sem, sem = refs
    run = (lax.axis_index("vir") // 2) ^ step
    copies = [
        pltpu.make_async_copy(amps_other, amps_here, come_sem.at[0]),
        pltpu.make_async_copy(ints_other, ints_here, come_sem.at[1]),
    ]

    def send(n, total):
        encode(total[...], stage.at[n])
        for out, (low, high) in zip(outs, pieces):

            @pl.when((n >= low) & (n < high))
            def _(out=out, low=low):
                pltpu.make_async_copy(stage.at[n], out.at[n - low], sem.at[n]).start()

    own, others = (amps_own, ints_own), (amps_here, ints_here)
    two_parts(size, wanted, run, mask_own, mask_other, own, others, copies, totals, wide, lambda tile, total: None, send)

    def finish(n, carry):
        @pl.when(wanted[n] >= 0)
        def _():
            pltpu.make_async_copy(stage.at[n], outs[0].at[0], sem.at[n]).wait()

        return carry

    lax.fori_loop(0, size.tiles, finish, 0)


def own_kernel(
    size, wanted, mask_own, mask_other, amps_own, ints_own, amps_other, ints_other, fock_vir, fock_occ, out, *refs
):
    totals, amps_here, ints_here, wide, come_sem, sem = refs
    run = lax.axis_index("vir") // 2
    copies = [
        pltpu.make_async_copy(amps_other, amps_here, come_sem.at[0]),
        pltpu.make_async_copy(ints_other, ints_here, come_sem.at[1]),
    ]

    def fock(tile, total):
        pair, column = tile // size.blocks, lax.rem(tile, size.blocks)

        @pl.when(((mask_own[pair] >> column) & 1) != 0)
        def _():
            amps = amps_own[tile]
            total[...] += jnp.dot(amps, fock_vir[column], preferred_element_type=jnp.float32)
            total[...] -= jnp.dot(fock_occ[pair], amps, preferred_element_type=jnp.float32)

    def send(n, total):
        pltpu.make_async_copy(total, out.at[n], sem.at[n]).start()

    own, others = (amps_own, ints_own), (amps_here, ints_here)
    two_parts(size, wanted, run, mask_own, mask_other, own, others, copies, totals, wide, fock, send)

    def finish(n, carry):
        @pl.when(wanted[n] >= 0)
        def _():
            pltpu.make_async_copy(totals.at[n], out.at[0], sem.at[n]).wait()

        return carry

    lax.fori_loop(0, size.tiles, finish, 0)


def join_kernel(size, chunk, pieces, others, late, spots, own, amps, *refs):
    came, refs = refs[: others * len(pieces)], refs[others * len(pieces) :]
    outs, refs = refs[:-8], refs[-8:]
    own_here, came_here, amps_here, stage, own_sem, came_sem, amps_sem, out_sem = refs
    per_dest = size.starts[chunk + 1] - size.starts[chunk]
    first, many = size.starts[chunk] * size.dests, per_dest * size.dests

    def fetch(n, carry):
        what, spot = late[first + n], spots[first + n]

        @pl.when((what >= 0) & (what < AMPS))
        def _():
            pltpu.make_async_copy(own.at[spot], own_here.at[n], own_sem.at[n]).start()
            for k in range(others):
                for piece, (low, high) in enumerate(pieces):

                    @pl.when((spot >= low) & (spot < high))
                    def _(k=k, piece=piece, low=low):
                        source = came[k * len(pieces) + piece]
                        pltpu.make_async_copy(source.at[spot - low], came_here.at[k, n], came_sem.at[k, n]).start()

        @pl.when(what >= AMPS)
        def _():
            pltpu.make_async_copy(amps.at[what - AMPS], amps_here.at[n], amps_sem.at[n]).start()

        return carry

    def send(n):
        if len(outs) == 1:
            target = outs[0].at[(n // per_dest) ^ lax.axis_index("occ"), lax.rem(n, per_dest)]
            pltpu.make_async_copy(stage.at[n], target, out_sem.at[n]).start()
            return
        for s in range(size.dests):

            @pl.when(n // per_dest == s)
            def _(s=s):
                slot = lax.rem(n, per_dest)
                pltpu.make_async_copy(stage.at[n], outs[s].at[slot], out_sem.at[n]).start()

    def make(n, carry):
        what = late[first + n]

        @pl.when((what >= 0) & (what < AMPS))
        def _():
            pltpu.make_async_copy(own.at[0], own_here.at[n], own_sem.at[n]).wait()
            total = own_here[n]
            for k in range(others):
                pltpu.make_async_copy(came[0].at[0], came_here.at[k, n], came_sem.at[k, n]).wait()
                total = total + decode(came_here[k, n])
            encode(total, stage.at[n])
            send(n)

        @pl.when(what >= AMPS)
        def _():
            pltpu.make_async_copy(amps.at[0], amps_here.at[n], amps_sem.at[n]).wait()
            encode(amps_here[n].astype(jnp.float32), stage.at[n])
            send(n)

        return carry

    def finish(n, carry):
        @pl.when(late[first + n] >= 0)
        def _():
            target = outs[0].at[0, 0] if len(outs) == 1 else outs[0].at[0]
            pltpu.make_async_copy(stage.at[n], target, out_sem.at[n]).wait()

        return carry

    lax.fori_loop(0, many, fetch, 0)
    lax.fori_loop(0, many, make, 0)
    lax.fori_loop(0, many, finish, 0)


def pack_kernel(size, table, amps, *refs):
    outs, (stage, come_sem, go_sem) = refs[: size.dests], refs[size.dests :]

    def each(act):
        for s in range(size.dests):
            for slot in range(size.extra):
                n = s * size.extra + slot

                @pl.when(table[n] >= 0)
                def _(s=s, slot=slot, n=n):
                    act(s, slot, n)

    def come(s, slot, n):
        return pltpu.make_async_copy(amps.at[jnp.maximum(table[n], 0)], stage.at[n], come_sem.at[n])

    def go(s, slot, n):
        return pltpu.make_async_copy(stage.at[n], outs[s].at[slot], go_sem.at[n])

    def turn(*at):
        come(*at).wait()
        go(*at).start()

    each(lambda *at: come(*at).start())
    each(turn)
    each(lambda *at: go(*at).wait())


def final_kernel(size, counts, with_extra, first, last, buffers, notes, occ_cols, vir_energy, amps, *refs):
    codes = []
    for count in counts:
        codes.append(refs[:count])
        refs = refs[count:]
    me = lax.axis_index("occ")
    one_code = codes[0][0].at[0] if counts[0] > 1 else codes[0][0].at[0, 0]
    one_amps = amps.at[0, pl.ds(0, size.rows)]
    more = refs[: size.dests] if with_extra else None
    out_res, out_upd, slot_of, col_of, row_of, kind_of, has_res, res_here, code_here, amps_here, made = refs[-14:-3]
    res_sem, amps_sem, go_sem = refs[-3:]
    rows, width = made.shape[2], made.shape[3]

    def fetch_code(s, slot, target, sem):
        for chunk, parts in enumerate(codes):

            @pl.when(chunk_of(size, slot) == chunk)
            def _(chunk=chunk, parts=parts):
                at = slot - size.starts[chunk]
                source = parts[s].at[at] if len(parts) > 1 else parts[0].at[s ^ me, at]
                pltpu.make_async_copy(source, target, sem).start()

    for s in range(size.dests):

        def fetch(n, carry, s=s):
            at = s * size.slots + n
            source = s ^ me
            owned, tile, res_slot, amp_slot = (notes[source, n * FIELDS + f] for f in range(FIELDS))
            amp_late = amp_slot - size.early
            is_late = (amp_late >= 0) & (amp_late < size.slots)
            is_extra = amp_late >= size.slots
            is_early = (amp_slot >= 0) & (amp_slot < size.early)
            needs = jnp.maximum(
                jnp.where(res_slot >= 0, chunk_of(size, res_slot), 0),
                jnp.where(is_extra, len(size.starts) - 2, jnp.where(is_late, chunk_of(size, amp_late), 0)),
            )
            mine = (owned > 0) & (needs >= first) & (needs <= last)
            slot_of[at] = jnp.where(mine, owned - 1, -1)
            pair = tile // size.blocks
            col_of[at] = source * size.pairs + pair
            row_of[at] = tile - pair * size.blocks
            kind_of[at] = jnp.where(is_late, 2, jnp.where(amp_slot >= 0, 1, 0))
            has_res[at] = (res_slot >= 0).astype(jnp.int32)

            @pl.when(mine & (res_slot >= 0))
            def _():
                fetch_code(s, res_slot, res_here.at[at], res_sem.at[at])

            @pl.when(mine & is_early)
            def _():
                place = pl.ds(pl.multiple_of(amp_slot * size.rows, 16), size.rows)
                pltpu.make_async_copy(amps.at[source, place], amps_here.at[at], amps_sem.at[at]).start()

            @pl.when(mine & is_late)
            def _():
                fetch_code(s, amp_late, code_here.at[at], amps_sem.at[at])

            if with_extra:

                @pl.when(mine & is_extra)
                def _():
                    spare = more[s].at[amp_late - size.slots]
                    pltpu.make_async_copy(spare, amps_here.at[at], amps_sem.at[at]).start()

            return carry

        lax.fori_loop(0, size.slots, fetch, 0)

    def leave(slot, buffer):
        return (
            pltpu.make_async_copy(made.at[buffer, 0], out_res.at[slot, 0], go_sem.at[buffer, 0]),
            pltpu.make_async_copy(made.at[buffer, 1], out_upd.at[slot, 0], go_sem.at[buffer, 1]),
        )

    def step(at, count):
        slot = slot_of[at]
        mine = slot >= 0
        buffer = lax.rem(count, buffers)

        @pl.when(mine)
        def _():
            @pl.when(count >= buffers)
            def _():
                for copy in leave(0, buffer):
                    copy.wait()

            kind = kind_of[at]

            @pl.when(kind == 0)
            def _():
                made[buffer, 1] = jnp.zeros((rows, width), jnp.float32)

            @pl.when(kind == 1)
            def _():
                pltpu.make_async_copy(one_amps, amps_here.at[at], amps_sem.at[at]).wait()
                made[buffer, 1] = amps_here[at].astype(jnp.float32)

            @pl.when(kind == 2)
            def _():
                pltpu.make_async_copy(one_code, code_here.at[at], amps_sem.at[at]).wait()
                made[buffer, 1] = decode(code_here[at])

            @pl.when(has_res[at] == 0)
            def _():
                made[buffer, 0] = jnp.zeros((rows, width), jnp.float32)

            @pl.when(has_res[at] != 0)
            def _():
                pltpu.make_async_copy(one_code, res_here.at[at], res_sem.at[at]).wait()
                resid = decode(res_here[at])
                lane = lax.broadcasted_iota(jnp.int32, (rows, width), 1)
                occ = jnp.sum(jnp.where(lane == col_of[at], occ_cols[...], 0.0), axis=1, keepdims=True)
                vir = vir_energy[pl.ds(row_of[at], 1), :]
                made[buffer, 0] = resid
                made[buffer, 1] += resid / (vir - occ)

            for copy in leave(slot, buffer):
                copy.start()

        return count + mine.astype(jnp.int32)

    count = lax.fori_loop(0, size.dests * size.slots, step, jnp.int32(0))
    for buffer in range(buffers):

        @pl.when(buffer < count)
        def _(buffer=buffer):
            for copy in leave(0, buffer):
                copy.wait()


def body(
    amplitudes,
    amp_keep,
    integrals,
    int_keep,
    fock_vir,
    fock_occ,
    occ_energy,
    vir_energy,
    res_keep,
    res_place,
):
    pairs, rows, blocks, width = amplitudes.shape
    dests, virs = lax.axis_size("occ"), lax.axis_size("vir")
    runs = virs // 2
    tiles = pairs * blocks
    slots = max(2, (tiles + dests - 1) // dests)
    early = max(1, 2 * slots // 3)
    starts = (0, slots // 3, slots * 2 // 3, slots) if slots % 3 == 0 else (0, 1, slots)
    chunks = len(starts) - 1
    entries = slots * dests
    size = Size(
        pairs, rows, blocks, width, dests, runs, tiles, slots, early, slots - early, starts, entries
    )
    coded = (rows + CODE_ROWS, width)
    plain = (rows, width)

    def swap(array, axis, bit):
        return lax.ppermute(array, axis, [(i, i ^ bit) for i in range(lax.axis_size(axis))])

    def words(count):
        return jax.ShapeDtypeStruct((count,), jnp.int32)

    def counters(count):
        return pltpu.SMEM((count,), jnp.int32)

    dma = pltpu.SemaphoreType.DMA

    amps = jnp.transpose(amplitudes, (0, 2, 1, 3)).reshape(tiles, rows, width)
    amps_other = swap(amps, "vir", 1)
    ints_other = swap(integrals, "vir", 1)

    sent_rows = early * rows + (PARTS + 1) * NOTE_ROWS
    late, spots, wanted, extra, mask_own, mask_send, packed = call(
        functools.partial(plan_kernel, size),
        "plan_tiles",
        (res_place, res_keep, amp_keep, int_keep, occ_energy, amps),
        [HBM] * 4 + [VMEM, HBM],
        [
            words(size.entries),
            words(size.entries),
            words(tiles),
            words(dests * size.extra),
            words(pairs + runs * blocks),
            words(pairs + runs * blocks),
            jax.ShapeDtypeStruct((dests, sent_rows, width), amps.dtype),
        ],
        [SMEM] * 6 + [HBM],
        [pltpu.SMEM(a.shape, jnp.int32) for a in (res_place, res_keep, amp_keep, int_keep)]
        + [dma((4,)), counters(dests * slots * FIELDS), counters(dests * early)]
        + [counters(dests)] * 3
        + [
            counters(dests + 1),
            pltpu.VMEM((dests * early, *plain), amps.dtype),
            pltpu.VMEM((NOTE_ROWS, width), jnp.float32),
            pltpu.VMEM((dests, (PARTS + 1) * NOTE_ROWS, width), amps.dtype),
            dma((dests * early,)),
            dma((dests * early,)),
            dma((dests,)),
        ],
        55,
    )
    wanted_other = [swap(wanted, "vir", 2 * k) for k in range(1, runs)]
    amps_came = lax.all_to_all(packed, "occ", split_axis=0, concat_axis=0, tiled=True)
    mask_other = swap(mask_send, "vir", 1)

    shared = (mask_own, mask_other, amps, integrals, amps_other, ints_other)
    share_specs = [SMEM] * 2 + [VMEM] * 2 + [HBM] * 2
    all_tiles = pltpu.VMEM((tiles, *plain), jnp.float32)
    other_core = [pltpu.VMEM(amps.shape, amps.dtype), pltpu.VMEM(integrals.shape, integrals.dtype)]
    other_core += [pltpu.VMEM((8 * width, width), jnp.float32), dma((2,))]

    bounds = [min(tiles, start * dests) for start in starts[1:-1]]
    bounds = sorted({0, *bounds, max(bounds[-1], tiles - tiles // 6), tiles})
    pieces = list(zip(bounds[:-1], bounds[1:]))
    rare = pieces[-1][0] >= tiles - tiles // 6 and len(pieces) > 1
    sums_came = []
    for k in range(1, runs):
        sums = call(
            functools.partial(sums_kernel, size, pieces, k),
            "ladder_sums",
            (wanted_other[k - 1], *shared),
            [SMEM] + share_specs,
            [jax.ShapeDtypeStruct((high - low, *coded), jnp.int16) for low, high in pieces],
            [HBM] * len(pieces),
            [all_tiles, pltpu.VMEM((tiles, *coded), jnp.int16), *other_core, dma((tiles,))],
            28,
        )
        came = [swap(part, "vir", 2 * k) for part in (sums[:-1] if rare else sums)]
        if rare:
            came.append(sums[-1])
        sums_came.append(came)

    buffers = 4
    own = call(
        functools.partial(own_kernel, size),
        "own_part",
        (wanted, *shared, fock_vir, fock_occ),
        [SMEM] + share_specs + [VMEM] * 2,
        jax.ShapeDtypeStruct((tiles, *plain), jnp.float32),
        HBM,
        [all_tiles, *other_core, dma((tiles,))],
        55,
    )

    if rare:
        for k in range(1, runs):
            beyond = (wanted[pieces[-1][0]] >= 0) | (wanted_other[k - 1][pieces[-1][0]] >= 0)
            part, _ = lax.optimization_barrier((sums_came[k - 1][-1], own))
            sums_came[k - 1][-1] = lax.cond(beyond, functools.partial(swap, axis="vir", bit=2 * k), lambda part: part, part)

    codes = []
    for c in range(chunks):
        use = pieces if c == chunks - 1 else pieces[: min(c + 1, len(pieces))]
        per_dest = starts[c + 1] - starts[c]
        per_chunk = per_dest * dests
        came = [part for parts in sums_came for part in parts[: len(use)]]
        if codes:
            late, _ = lax.optimization_barrier((late, joined[0]))
        spread = True
        outs = dests if spread else 1
        joined = call(
            functools.partial(join_kernel, size, c, use, runs - 1),
            "join_parts",
            (late, spots, own, amps, *came),
            [SMEM] * 2 + [HBM] * (2 + len(came)),
            [jax.ShapeDtypeStruct((per_dest, *coded) if spread else (dests, per_dest, *coded), jnp.int16)] * outs,
            [HBM] * outs,
            [
                pltpu.VMEM((per_chunk, *plain), jnp.float32),
                pltpu.VMEM((runs - 1, per_chunk, *coded), jnp.int16),
                pltpu.VMEM((per_chunk, *plain), amps.dtype),
                pltpu.VMEM((per_chunk, *coded), jnp.int16),
                dma((per_chunk,)),
                dma((runs - 1, per_chunk)),
                dma((per_chunk,)),
                dma((per_chunk,)),
            ],
            60,
        )
        if spread:
            codes.append([joined[0]] + [swap(joined[s], "occ", s) for s in range(1, dests)])
        else:
            codes.append([lax.all_to_all(joined[0], "occ", split_axis=0, concat_axis=0, tiled=True)])

    amps_came, _ = lax.optimization_barrier((amps_came, codes[0][0]))
    said = amps_came[:, early * rows :].reshape(dests, PARTS + 1, NOTE_ROWS, width).astype(jnp.float32)
    strips = -(-rows // width)
    occ_all = (said[:, 0] + said[:, 1] + said[:, 2])[:, : pairs * strips].reshape(dests * pairs, strips * width)[:, :rows]
    occ_cols = jnp.transpose(jnp.pad(occ_all, ((0, width - dests * pairs), (0, 0))))
    notes = said[:, PARTS, 0].astype(jnp.int32)
    over = jnp.max(notes[:, slots * FIELDS]) > 0

    def finish(first, last, more, results):
        have = [code for part in codes[: last + 1] for code in part]
        inputs = (notes, occ_cols, vir_energy, amps_came, *have, *more, *results)
        counts = tuple(len(part) for part in codes[: last + 1])
        many = dests * slots
        return call(
            functools.partial(final_kernel, size, counts, bool(more), first, last, buffers),
            "update_tiles",
            inputs,
            [SMEM] + [VMEM] * 2 + [HBM] * (len(inputs) - 3),
            [jax.ShapeDtypeStruct((tiles, 1, *plain), jnp.float32)] * 2,
            [HBM] * 2,
            [counters(many)] * 5
            + [
                pltpu.VMEM((many, *coded), jnp.int16),
                pltpu.VMEM((many, *coded), jnp.int16),
                pltpu.VMEM((many, *plain), amps.dtype),
                pltpu.VMEM((buffers, 2, *plain), jnp.float32),
                dma((many,)),
                dma((many,)),
                dma((buffers, 2)),
            ],
            60,
            {len(inputs) - 2: 0, len(inputs) - 1: 1} if results else None,
        )

    results = finish(0, 0, [], ())

    def with_extra(results):
        more = call(
            functools.partial(pack_kernel, size),
            "pack_extra",
            (extra, amps),
            [SMEM, HBM],
            [jax.ShapeDtypeStruct((size.extra, *plain), amps.dtype)] * dests,
            [HBM] * dests,
            [
                pltpu.VMEM((dests * size.extra, *plain), amps.dtype),
                dma((dests * size.extra,)),
                dma((dests * size.extra,)),
            ],
            60,
        )
        more = [more[0]] + [swap(more[s], "occ", s) for s in range(1, dests)]
        return tuple(finish(1, chunks - 1, more, results))

    def without_extra(results):
        return tuple(finish(1, chunks - 1, [], results))

    return lax.cond(over, with_extra, without_extra, tuple(results))


def solution(mesh):
    return jax.shard_map(
        body,
        mesh=mesh,
        in_specs=(
            P(("groups", "occ"), None, "vir", None),
            P(("groups", "occ"), "vir"),
            P(("groups", "vir"), None, None, None),
            P(("groups", "vir"), None),
            P(("groups", "vir"), None, None),
            P(("groups", "occ"), None, None),
            P(("groups", "occ"), None),
            P(("groups", "vir"), None),
            P(("groups", "occ"), "vir"),
            P(("groups", "occ"), "vir"),
        ),
        out_specs=(
            P(("groups", "occ"), "vir", None, None),
            P(("groups", "occ"), "vir", None, None),
        ),
        check_vma=False,
    )
```

```python
import collections
import functools

import jax
import jax.numpy as jnp
from jax import lax
from jax.experimental import pallas as pl
from jax.experimental.pallas import tpu as pltpu
from jax.sharding import PartitionSpec as P

CODE_ROWS = 16
LEVELS = 32700.0
MIB = 1024 * 1024
AMPS = 1024
FIELDS = 4
NOTE_ROWS = 16
PARTS = 3
HBM = pl.BlockSpec(memory_space=pltpu.HBM)
SMEM = pl.BlockSpec(memory_space=pltpu.SMEM)
VMEM = pl.BlockSpec(memory_space=pltpu.VMEM)
SIZE_NAMES = ("pairs", "rows", "blocks", "width", "dests", "runs", "tiles", "slots", "early", "extra")
SIZE_NAMES += ("starts", "entries")
Size = collections.namedtuple("Size", SIZE_NAMES)


def call(kernel, name, inputs, in_specs, out_shape, out_specs, scratch, vmem, aliases=None):
    return pl.pallas_call(
        kernel,
        out_shape=out_shape,
        in_specs=in_specs,
        out_specs=out_specs,
        scratch_shapes=scratch,
        input_output_aliases=aliases or {},
        compiler_params=pltpu.CompilerParams(vmem_limit_bytes=vmem * MIB),
        name=name,
    )(*inputs)


def chunk_of(size, slot):
    return sum((slot >= start).astype(jnp.int32) for start in size.starts[1:-1])


def scale_block(rows):
    return 80 if rows % 80 == 0 else rows


def encode(values, out):
    rows, width = values.shape
    block = scale_block(rows)
    cut = values.reshape(rows // block, block, width)
    top = jnp.max(jnp.abs(cut), axis=1, keepdims=True)
    step = jnp.clip(jnp.ceil(8.0 * jnp.log2(jnp.maximum(top, 1e-30))), -800.0, 800.0)
    whole = jnp.round(cut * (LEVELS * jnp.exp2(step * -0.125))).reshape(rows, width)
    out[:rows, :] = whole.astype(jnp.int32).astype(jnp.int16)
    steps = step.reshape(rows // block, width)
    steps = jnp.concatenate([steps, jnp.zeros((CODE_ROWS - rows // block, width), jnp.float32)], axis=0)
    out[rows:, :] = steps.astype(jnp.int32).astype(jnp.int16)


def decode(coded):
    rows, width = coded.shape[0] - CODE_ROWS, coded.shape[1]
    block = scale_block(rows)
    steps = coded[rows:, :].astype(jnp.int32).astype(jnp.float32)[: rows // block]
    scale = jnp.exp2(steps * 0.125) * (1.0 / LEVELS)
    whole = coded[:rows, :].astype(jnp.int32).astype(jnp.float32)
    return (whole.reshape(rows // block, block, width) * scale.reshape(rows // block, 1, width)).reshape(rows, width)


def plan_kernel(size, place_in, res_keep_in, amp_keep_in, int_keep_in, occ_energy, amps, *refs):
    late, spots, wanted, extra, mask_own, mask_send, packed = refs[:7]
    place, res_keep, amp_keep, int_keep, word_sem = refs[7:12]
    notes, early_at, res_count, amp_count, all_count, res_seen, stage, energies, note, come_sem, go_sem, note_sem = refs[12:]
    words_in = [
        pltpu.make_async_copy(source, target, word_sem.at[n])
        for n, (source, target) in enumerate(
            ((place_in, place), (res_keep_in, res_keep), (amp_keep_in, amp_keep), (int_keep_in, int_keep))
        )
    ]
    for copy in words_in:
        copy.start()
    me, core = lax.axis_index("occ"), lax.rem(lax.axis_index("vir"), 2)

    for s in range(size.dests):
        for ref in (res_count, amp_count, all_count, res_seen):
            ref[s] = 0
    for n in range(size.dests * size.extra):
        extra[n] = -1
    for n in range(size.dests * size.early):
        early_at[n] = -1

    def clear(n, carry):
        late[n] = -1
        spots[n] = 0
        for f in range(FIELDS):
            notes[n * FIELDS + f] = 0
        return carry

    lax.fori_loop(0, size.entries, clear, 0)
    for n in range(size.tiles):
        wanted[n] = -1
    for copy in words_in:
        copy.wait()

    res_seen[size.dests] = 0

    def entry(s, slot):
        at = s * size.starts[1] + slot
        for low, high in zip(size.starts[1:-1], size.starts[2:]):
            at = jnp.where(slot >= low, low * size.dests + s * (high - low) + slot - low, at)
        return at

    def aim(pair, column):
        where = place[pair, column]
        target = sum((where >= n * size.tiles).astype(jnp.int32) for n in range(1, size.dests))
        return target ^ me, where - target * size.tiles

    def residuals(pair, carry):
        for column in range(size.blocks):
            s, _ = aim(pair, column)

            @pl.when(res_keep[pair, column] != 0)
            def _(column=column, s=s):
                slot = res_count[s]
                res_count[s] = slot + 1
                late[entry(s, slot)] = pair * size.blocks + column

        return carry

    lax.fori_loop(0, size.pairs, residuals, 0)

    def amplitudes(pair, carry):
        for column in range(size.blocks):
            tile = pair * size.blocks + column
            s, owned = aim(pair, column)
            first = (s * size.slots + all_count[s]) * FIELDS
            all_count[s] = all_count[s] + 1
            notes[first] = owned + 1
            notes[first + 1] = tile
            notes[first + 2] = -1
            notes[first + 3] = -1

            @pl.when(res_keep[pair, column] != 0)
            def _(s=s, first=first):
                notes[first + 2] = res_seen[s]
                res_seen[s] = res_seen[s] + 1

            @pl.when(amp_keep[pair, column] != 0)
            def _(s=s, first=first, tile=tile):
                rank = amp_count[s]
                amp_count[s] = rank + 1
                slot = size.slots - 1 - (rank - size.early)

                @pl.when(rank < size.early)
                def _():
                    n = s * size.early + rank
                    early_at[n] = tile
                    notes[first + 3] = rank
                    pltpu.make_async_copy(amps.at[tile], stage.at[n], come_sem.at[n]).start()

                @pl.when((rank >= size.early) & (slot >= res_count[s]))
                def _():
                    late[entry(s, slot)] = tile + AMPS
                    notes[first + 3] = size.early + slot

                @pl.when((rank >= size.early) & (slot < res_count[s]))
                def _():
                    extra[s * size.extra + rank - size.early] = tile
                    notes[first + 3] = size.slots + rank
                    res_seen[size.dests] = 1

        return carry

    lax.fori_loop(0, size.pairs, amplitudes, 0)

    for s in range(size.dests):
        for slot in range(size.early):
            n = s * size.early + slot

            @pl.when(early_at[n] >= 0)
            def _(s=s, slot=slot, n=n):
                rows = pl.ds(slot * size.rows, size.rows)
                pltpu.make_async_copy(amps.at[0], stage.at[n], come_sem.at[n]).wait()
                pltpu.make_async_copy(stage.at[n], packed.at[me ^ s, rows], go_sem.at[n]).start()

    energies[...] = jnp.zeros((NOTE_ROWS, size.width), jnp.float32)
    strips = -(-size.rows // size.width)
    for pair in range(size.pairs):
        for strip in range(strips):
            low, high = strip * size.width, min(size.rows, (strip + 1) * size.width)
            energies[pair * strips + strip : pair * strips + strip + 1, : high - low] = occ_energy[pair : pair + 1, low:high]
    left = energies[...]
    lane = lax.broadcasted_iota(jnp.int32, (NOTE_ROWS, size.width), 1)
    parts = []
    for _ in range(PARTS):
        parts.append(left.astype(jnp.bfloat16))
        left = left - parts[-1].astype(jnp.float32)
    for s in range(size.dests):
        for n, part in enumerate(parts):
            note[s, n * NOTE_ROWS : (n + 1) * NOTE_ROWS] = part
        words = jnp.where(lane == size.slots * FIELDS, res_seen[size.dests], 0)
        for n in range(size.slots * FIELDS):
            words = jnp.where(lane == n, notes[s * size.slots * FIELDS + n], words)
        note[s, PARTS * NOTE_ROWS :] = words.astype(jnp.float32).astype(jnp.bfloat16)
        target = packed.at[me ^ s, pl.ds(size.early * size.rows, (PARTS + 1) * NOTE_ROWS)]
        pltpu.make_async_copy(note.at[s], target, note_sem.at[s]).start()

    def compact(n, count):
        what = late[n]
        kept = (what >= 0) & (what < AMPS)

        @pl.when(kept)
        def _():
            wanted[count] = what
            spots[n] = count

        return count + kept.astype(jnp.int32)

    lax.fori_loop(0, size.entries, compact, jnp.int32(0))

    for pair in range(size.pairs):
        mask = amp_keep[pair, 0]
        for block in range(1, size.blocks):
            mask = mask | (amp_keep[pair, block] << block)
        mask_own[pair] = mask
        mask_send[pair] = mask

    def integrals(run, carry):
        for column in range(size.blocks):
            for target, parity in ((mask_own, core), (mask_send, 1 - core)):
                at = (run * 2 + parity) * size.blocks + column
                mask = int_keep[0, at]
                for block in range(1, size.blocks):
                    mask = mask | (int_keep[block, at] << block)
                target[size.pairs + run * size.blocks + column] = mask
        return carry

    lax.fori_loop(0, size.runs, integrals, 0)

    for s in range(size.dests):
        for slot in range(size.early):
            n = s * size.early + slot

            @pl.when(early_at[n] >= 0)
            def _(s=s, slot=slot, n=n):
                pltpu.make_async_copy(stage.at[n], packed.at[0, pl.ds(0, size.rows)], go_sem.at[n]).wait()

        target = packed.at[0, pl.ds(0, (PARTS + 1) * NOTE_ROWS)]
        pltpu.make_async_copy(note.at[s], target, note_sem.at[s]).wait()


def integral_tile(ints, place, wide):
    for first in range(0, ints.shape[1], 8):

        @pl.when((place >= first) & (place < first + 8))
        def _(first=first):
            part = ints[:, first : first + 8, :].astype(jnp.float32)
            wide[...] = part.reshape(wide.shape)

    return wide[pl.ds(lax.rem(place, 8), ints.shape[0], stride=8), :].astype(ints.dtype)


def ladder(size, span, wanted, run, masks, sources, totals, work, more, last):
    active, amps, ints, wide, amp_sem, int_sem = work
    amp_copies, int_copies = [], []
    for part in range(2):
        amp_copies.append(pltpu.make_async_copy(sources[2 * part], amps.at[part], amp_sem.at[part]))
        amp_copies[-1].start()
        int_copies.append([])
        for block in range(size.blocks):
            source = sources[2 * part + 1].at[block]
            int_copies[-1].append(pltpu.make_async_copy(source, ints.at[part, block], int_sem.at[part, block]))
            int_copies[-1][-1].start()
    core = lax.rem(lax.axis_index("vir"), 2)

    def prepare(n, carry):
        tile = wanted[n]
        active[n] = 0

        @pl.when(tile >= 0)
        def _():
            pair, column = tile // size.blocks, lax.rem(tile, size.blocks)
            at = size.pairs + run * size.blocks + column
            both = (masks[0][pair] & masks[0][at]) | ((masks[1][pair] & masks[1][at]) << size.blocks)
            active[n] = both
            totals[n] = jnp.zeros((size.rows, size.width), jnp.float32)

        return carry

    lax.fori_loop(*span, prepare, 0)
    for part in range(2):
        amp_copies[part].wait()
        if part == 0 and more is not None:

            def add_more(n, carry):
                @pl.when(wanted[n] >= 0)
                def _():
                    more(wanted[n], totals.at[n], amps.at[0])

                return carry

            lax.fori_loop(*span, add_more, 0)
        for block in range(size.blocks):
            int_copies[part][block].wait()
            bit = 1 << (part * size.blocks + block)

            def add(n, carry, part=part, block=block, bit=bit):
                @pl.when((active[n] & bit) != 0)
                def _():
                    tile = wanted[n]
                    pair, column = tile // size.blocks, lax.rem(tile, size.blocks)
                    place = (run * 2 + core) * size.blocks + column
                    totals[n] += jnp.dot(
                        amps[part, pair * size.blocks + block],
                        integral_tile(ints.at[part, block], place, wide),
                        preferred_element_type=jnp.float32,
                    )

                return carry

            lax.fori_loop(*span, add, 0)

    def leave(n, carry):
        @pl.when(wanted[n] >= 0)
        def _():
            last(n, totals.at[n])

        return carry

    lax.fori_loop(*span, leave, 0)


def sums_kernel(size, pieces, step, wanted, mask_own, mask_other, amps_own, ints_own, amps_other, ints_other, *refs):
    outs, refs = refs[: len(pieces)], refs[len(pieces) :]
    totals, work, (stage, sem) = refs[0], refs[1:7], refs[7:]
    run = (lax.axis_index("vir") // 2) ^ step
    span = (pieces[0][0], pieces[-1][1])

    def send(n, total):
        encode(total[...], stage.at[n])
        for out, (low, high) in zip(outs, pieces):

            @pl.when((n >= low) & (n < high))
            def _(out=out, low=low):
                pltpu.make_async_copy(stage.at[n], out.at[n - low], sem.at[n]).start()

    sources = (amps_own, ints_own, amps_other, ints_other)
    ladder(size, span, wanted, run, (mask_own, mask_other), sources, totals, work, None, send)

    def finish(n, carry):
        @pl.when(wanted[n] >= 0)
        def _():
            pltpu.make_async_copy(stage.at[n], outs[0].at[0], sem.at[n]).wait()

        return carry

    lax.fori_loop(*span, finish, 0)


def own_kernel(
    size, span, wanted, mask_own, mask_other, amps_own, ints_own, amps_other, ints_other, fock_vir, fock_occ, out, *refs
):
    totals, work, sem = refs[0], refs[1:7], refs[7]
    run = lax.axis_index("vir") // 2

    def fock(tile, total, amps):
        pair, column = tile // size.blocks, lax.rem(tile, size.blocks)

        @pl.when(((mask_own[pair] >> column) & 1) != 0)
        def _():
            kept = amps[tile]
            total[...] += jnp.dot(kept, fock_vir[column], preferred_element_type=jnp.float32)
            total[...] -= jnp.dot(fock_occ[pair], kept, preferred_element_type=jnp.float32)

    def send(n, total):
        pltpu.make_async_copy(total, out.at[n - span[0]], sem.at[n]).start()

    sources = (amps_own, ints_own, amps_other, ints_other)
    ladder(size, span, wanted, run, (mask_own, mask_other), sources, totals, work, fock, send)

    def finish(n, carry):
        @pl.when(wanted[n] >= 0)
        def _():
            pltpu.make_async_copy(totals.at[n], out.at[0], sem.at[n]).wait()

        return carry

    lax.fori_loop(*span, finish, 0)


def join_kernel(size, chunk, pieces, own_spans, others, late, spots, amps, *refs):
    own, refs = refs[: len(own_spans)], refs[len(own_spans) :]
    came, refs = refs[: others * len(pieces)], refs[others * len(pieces) :]
    outs, refs = refs[:-8], refs[-8:]
    own_here, came_here, amps_here, stage, own_sem, came_sem, amps_sem, out_sem = refs
    per_dest = size.starts[chunk + 1] - size.starts[chunk]
    first, many = size.starts[chunk] * size.dests, per_dest * size.dests

    def fetch(n, carry):
        what, spot = late[first + n], spots[first + n]

        @pl.when((what >= 0) & (what < AMPS))
        def _():
            for part, (low, high) in zip(own, own_spans):

                @pl.when((spot >= low) & (spot < high))
                def _(part=part, low=low):
                    pltpu.make_async_copy(part.at[spot - low], own_here.at[n], own_sem.at[n]).start()

            for k in range(others):
                for piece, (low, high) in enumerate(pieces):

                    @pl.when((spot >= low) & (spot < high))
                    def _(k=k, piece=piece, low=low):
                        source = came[k * len(pieces) + piece]
                        pltpu.make_async_copy(source.at[spot - low], came_here.at[k, n], came_sem.at[k, n]).start()

        @pl.when(what >= AMPS)
        def _():
            pltpu.make_async_copy(amps.at[what - AMPS], amps_here.at[n], amps_sem.at[n]).start()

        return carry

    def send(n):
        if len(outs) == 1:
            target = outs[0].at[(n // per_dest) ^ lax.axis_index("occ"), lax.rem(n, per_dest)]
            pltpu.make_async_copy(stage.at[n], target, out_sem.at[n]).start()
            return
        for s in range(size.dests):

            @pl.when(n // per_dest == s)
            def _(s=s):
                slot = lax.rem(n, per_dest)
                pltpu.make_async_copy(stage.at[n], outs[s].at[slot], out_sem.at[n]).start()

    def make(n, carry):
        what = late[first + n]

        @pl.when((what >= 0) & (what < AMPS))
        def _():
            pltpu.make_async_copy(own[0].at[0], own_here.at[n], own_sem.at[n]).wait()
            total = own_here[n]
            for k in range(others):
                pltpu.make_async_copy(came[0].at[0], came_here.at[k, n], came_sem.at[k, n]).wait()
                total = total + decode(came_here[k, n])
            encode(total, stage.at[n])
            send(n)

        @pl.when(what >= AMPS)
        def _():
            pltpu.make_async_copy(amps.at[0], amps_here.at[n], amps_sem.at[n]).wait()
            encode(amps_here[n].astype(jnp.float32), stage.at[n])
            send(n)

        return carry

    def finish(n, carry):
        @pl.when(late[first + n] >= 0)
        def _():
            target = outs[0].at[0, 0] if len(outs) == 1 else outs[0].at[0]
            pltpu.make_async_copy(stage.at[n], target, out_sem.at[n]).wait()

        return carry

    lax.fori_loop(0, many, fetch, 0)
    lax.fori_loop(0, many, make, 0)
    lax.fori_loop(0, many, finish, 0)


def pack_kernel(size, table, amps, *refs):
    outs, (stage, come_sem, go_sem) = refs[: size.dests], refs[size.dests :]

    def each(act):
        for s in range(size.dests):
            for slot in range(size.extra):
                n = s * size.extra + slot

                @pl.when(table[n] >= 0)
                def _(s=s, slot=slot, n=n):
                    act(s, slot, n)

    def come(s, slot, n):
        return pltpu.make_async_copy(amps.at[jnp.maximum(table[n], 0)], stage.at[n], come_sem.at[n])

    def go(s, slot, n):
        return pltpu.make_async_copy(stage.at[n], outs[s].at[slot], go_sem.at[n])

    def turn(*at):
        come(*at).wait()
        go(*at).start()

    each(lambda *at: come(*at).start())
    each(turn)
    each(lambda *at: go(*at).wait())


def final_kernel(size, counts, with_extra, first, last, buffers, notes, occ_cols, vir_energy, amps, *refs):
    codes = []
    for count in counts:
        codes.append(refs[:count])
        refs = refs[count:]
    me = lax.axis_index("occ")
    one_code = codes[0][0].at[0] if counts[0] > 1 else codes[0][0].at[0, 0]
    one_amps = amps.at[0, pl.ds(0, size.rows)]
    more = refs[: size.dests] if with_extra else None
    out_res, out_upd, slot_of, col_of, row_of, kind_of, has_res, res_here, code_here, amps_here, made = refs[-14:-3]
    res_sem, amps_sem, go_sem = refs[-3:]
    rows, width = made.shape[2], made.shape[3]

    def fetch_code(s, slot, target, sem):
        for chunk, parts in enumerate(codes):

            @pl.when(chunk_of(size, slot) == chunk)
            def _(chunk=chunk, parts=parts):
                at = slot - size.starts[chunk]
                source = parts[s].at[at] if len(parts) > 1 else parts[0].at[s ^ me, at]
                pltpu.make_async_copy(source, target, sem).start()

    for s in range(size.dests):

        def fetch(n, carry, s=s):
            at = s * size.slots + n
            source = s ^ me
            owned, tile, res_slot, amp_slot = (notes[source, n * FIELDS + f] for f in range(FIELDS))
            amp_late = amp_slot - size.early
            is_late = (amp_late >= 0) & (amp_late < size.slots)
            is_extra = amp_late >= size.slots
            is_early = (amp_slot >= 0) & (amp_slot < size.early)
            needs = jnp.maximum(
                jnp.where(res_slot >= 0, chunk_of(size, res_slot), 0),
                jnp.where(is_extra, len(size.starts) - 2, jnp.where(is_late, chunk_of(size, amp_late), 0)),
            )
            mine = (owned > 0) & (needs >= first) & (needs <= last)
            slot_of[at] = jnp.where(mine, owned - 1, -1)
            pair = tile // size.blocks
            col_of[at] = source * size.pairs + pair
            row_of[at] = tile - pair * size.blocks
            kind_of[at] = jnp.where(is_late, 2, jnp.where(amp_slot >= 0, 1, 0))
            has_res[at] = (res_slot >= 0).astype(jnp.int32)

            @pl.when(mine & (res_slot >= 0))
            def _():
                fetch_code(s, res_slot, res_here.at[at], res_sem.at[at])

            @pl.when(mine & is_early)
            def _():
                place = pl.ds(pl.multiple_of(amp_slot * size.rows, 16), size.rows)
                pltpu.make_async_copy(amps.at[source, place], amps_here.at[at], amps_sem.at[at]).start()

            @pl.when(mine & is_late)
            def _():
                fetch_code(s, amp_late, code_here.at[at], amps_sem.at[at])

            if with_extra:

                @pl.when(mine & is_extra)
                def _():
                    spare = more[s].at[amp_late - size.slots]
                    pltpu.make_async_copy(spare, amps_here.at[at], amps_sem.at[at]).start()

            return carry

        lax.fori_loop(0, size.slots, fetch, 0)

    def leave(slot, buffer):
        return (
            pltpu.make_async_copy(made.at[buffer, 0], out_res.at[slot, 0], go_sem.at[buffer, 0]),
            pltpu.make_async_copy(made.at[buffer, 1], out_upd.at[slot, 0], go_sem.at[buffer, 1]),
        )

    def step(at, count):
        slot = slot_of[at]
        mine = slot >= 0
        buffer = lax.rem(count, buffers)

        @pl.when(mine)
        def _():
            @pl.when(count >= buffers)
            def _():
                for copy in leave(0, buffer):
                    copy.wait()

            kind = kind_of[at]

            @pl.when(kind == 0)
            def _():
                made[buffer, 1] = jnp.zeros((rows, width), jnp.float32)

            @pl.when(kind == 1)
            def _():
                pltpu.make_async_copy(one_amps, amps_here.at[at], amps_sem.at[at]).wait()
                made[buffer, 1] = amps_here[at].astype(jnp.float32)

            @pl.when(kind == 2)
            def _():
                pltpu.make_async_copy(one_code, code_here.at[at], amps_sem.at[at]).wait()
                made[buffer, 1] = decode(code_here[at])

            @pl.when(has_res[at] == 0)
            def _():
                made[buffer, 0] = jnp.zeros((rows, width), jnp.float32)

            @pl.when(has_res[at] != 0)
            def _():
                pltpu.make_async_copy(one_code, res_here.at[at], res_sem.at[at]).wait()
                resid = decode(res_here[at])
                lane = lax.broadcasted_iota(jnp.int32, (rows, width), 1)
                occ = jnp.sum(jnp.where(lane == col_of[at], occ_cols[...], 0.0), axis=1, keepdims=True)
                vir = vir_energy[pl.ds(row_of[at], 1), :]
                made[buffer, 0] = resid
                made[buffer, 1] += resid / (vir - occ)

            for copy in leave(slot, buffer):
                copy.start()

        return count + mine.astype(jnp.int32)

    count = lax.fori_loop(0, size.dests * size.slots, step, jnp.int32(0))
    for buffer in range(buffers):

        @pl.when(buffer < count)
        def _(buffer=buffer):
            for copy in leave(0, buffer):
                copy.wait()


def body(
    amplitudes,
    amp_keep,
    integrals,
    int_keep,
    fock_vir,
    fock_occ,
    occ_energy,
    vir_energy,
    res_keep,
    res_place,
):
    pairs, rows, blocks, width = amplitudes.shape
    dests, virs = lax.axis_size("occ"), lax.axis_size("vir")
    runs = virs // 2
    tiles = pairs * blocks
    slots = max(2, (tiles + dests - 1) // dests)
    early = max(1, 2 * slots // 3)
    starts = (0, slots // 3, slots * 2 // 3, slots) if slots % 3 == 0 else (0, 1, slots)
    chunks = len(starts) - 1
    entries = slots * dests
    size = Size(
        pairs, rows, blocks, width, dests, runs, tiles, slots, early, slots - early, starts, entries
    )
    coded = (rows + CODE_ROWS, width)
    plain = (rows, width)

    def swap(array, axis, bit):
        return lax.ppermute(array, axis, [(i, i ^ bit) for i in range(lax.axis_size(axis))])

    def words(count):
        return jax.ShapeDtypeStruct((count,), jnp.int32)

    def counters(count):
        return pltpu.SMEM((count,), jnp.int32)

    dma = pltpu.SemaphoreType.DMA

    amps = jnp.transpose(amplitudes, (0, 2, 1, 3)).reshape(tiles, rows, width)
    amps_other = swap(amps, "vir", 1)
    ints_other = swap(integrals, "vir", 1)

    sent_rows = early * rows + (PARTS + 1) * NOTE_ROWS
    late, spots, wanted, extra, mask_own, mask_send, packed = call(
        functools.partial(plan_kernel, size),
        "plan_tiles",
        (res_place, res_keep, amp_keep, int_keep, occ_energy, amps),
        [HBM] * 4 + [VMEM, HBM],
        [
            words(size.entries),
            words(size.entries),
            words(tiles),
            words(dests * size.extra),
            words(pairs + runs * blocks),
            words(pairs + runs * blocks),
            jax.ShapeDtypeStruct((dests, sent_rows, width), amps.dtype),
        ],
        [SMEM] * 6 + [HBM],
        [pltpu.SMEM(a.shape, jnp.int32) for a in (res_place, res_keep, amp_keep, int_keep)]
        + [dma((4,)), counters(dests * slots * FIELDS), counters(dests * early)]
        + [counters(dests)] * 3
        + [
            counters(dests + 1),
            pltpu.VMEM((dests * early, *plain), amps.dtype),
            pltpu.VMEM((NOTE_ROWS, width), jnp.float32),
            pltpu.VMEM((dests, (PARTS + 1) * NOTE_ROWS, width), amps.dtype),
            dma((dests * early,)),
            dma((dests * early,)),
            dma((dests,)),
        ],
        55,
    )
    wanted_other = [swap(wanted, "vir", 2 * k) for k in range(1, runs)]
    amps_came = lax.all_to_all(packed, "occ", split_axis=0, concat_axis=0, tiled=True)
    mask_other = swap(mask_send, "vir", 1)

    shared = (mask_own, mask_other, amps, integrals, amps_other, ints_other)
    share_specs = [SMEM] * 2 + [HBM] * 4
    work = [
        pltpu.VMEM((tiles, *plain), jnp.float32),
        counters(tiles),
        pltpu.VMEM((2, *amps.shape), amps.dtype),
        pltpu.VMEM((2, *integrals.shape), integrals.dtype),
        pltpu.VMEM((8 * width, width), jnp.float32),
        dma((2,)),
        dma((2, blocks)),
    ]

    bounds = [min(tiles, start * dests) for start in starts[1:-1]]
    bounds = sorted({0, *bounds, max(bounds[-1], tiles - tiles // 6), tiles})
    pieces = list(zip(bounds[:-1], bounds[1:]))
    rare = pieces[-1][0] >= tiles - tiles // 6 and len(pieces) > 1
    sums_came = []
    for k in range(1, runs):
        sums = []
        for some in (pieces[:1], pieces[1:]):
            if some:
                sums += call(
                    functools.partial(sums_kernel, size, some, k),
                    "ladder_sums",
                    (wanted_other[k - 1], *shared),
                    [SMEM] + share_specs,
                    [jax.ShapeDtypeStruct((high - low, *coded), jnp.int16) for low, high in some],
                    [HBM] * len(some),
                    [*work, pltpu.VMEM((tiles, *coded), jnp.int16), dma((tiles,))],
                    55,
                )
        came = [swap(part, "vir", 2 * k) for part in (sums[:-1] if rare else sums)]
        if rare:
            came.append(sums[-1])
        sums_came.append(came)

    def own_part(span, wanted):
        return call(
            functools.partial(own_kernel, size, span),
            "own_part",
            (wanted, *shared, fock_vir, fock_occ),
            [SMEM] + share_specs + [VMEM] * 2,
            jax.ShapeDtypeStruct((span[1] - span[0], *plain), jnp.float32),
            HBM,
            [*work, dma((tiles,))],
            55,
        )

    buffers = 4
    own_spans = [pieces[0]] + ([(pieces[0][1], tiles)] if len(pieces) > 1 else [])
    own = [own_part(own_spans[0], wanted)]

    codes = []
    for c in range(chunks):
        use = pieces if c == chunks - 1 else pieces[: min(c + 1, len(pieces))]
        per_dest = starts[c + 1] - starts[c]
        per_chunk = per_dest * dests
        if rare and c == chunks - 1:
            for k in range(1, runs):
                part, mine, theirs, _ = lax.optimization_barrier((sums_came[k - 1][-1], wanted, wanted_other[k - 1], joined[0]))
                beyond = (mine[use[-1][0]] >= 0) | (theirs[use[-1][0]] >= 0)
                sums_came[k - 1][-1] = lax.cond(
                    beyond, functools.partial(swap, axis="vir", bit=2 * k), lambda part: part, part
                )
        came = [part for parts in sums_came for part in parts[: len(use)]]
        if codes:
            late, after, _ = lax.optimization_barrier((late, wanted, joined[0]))
            if len(own) < len(own_spans):
                own.append(own_part(own_spans[1], after))
        spread = True
        outs = dests if spread else 1
        joined = call(
            functools.partial(join_kernel, size, c, use, own_spans[: len(own)], runs - 1),
            "join_parts",
            (late, spots, amps, *own, *came),
            [SMEM] * 2 + [HBM] * (1 + len(own) + len(came)),
            [jax.ShapeDtypeStruct((per_dest, *coded) if spread else (dests, per_dest, *coded), jnp.int16)] * outs,
            [HBM] * outs,
            [
                pltpu.VMEM((per_chunk, *plain), jnp.float32),
                pltpu.VMEM((runs - 1, per_chunk, *coded), jnp.int16),
                pltpu.VMEM((per_chunk, *plain), amps.dtype),
                pltpu.VMEM((per_chunk, *coded), jnp.int16),
                dma((per_chunk,)),
                dma((runs - 1, per_chunk)),
                dma((per_chunk,)),
                dma((per_chunk,)),
            ],
            60,
        )
        if spread:
            codes.append([joined[0]] + [swap(joined[s], "occ", s) for s in range(1, dests)])
        else:
            codes.append([lax.all_to_all(joined[0], "occ", split_axis=0, concat_axis=0, tiled=True)])

    amps_came, _ = lax.optimization_barrier((amps_came, codes[0][0]))
    said = amps_came[:, early * rows :].reshape(dests, PARTS + 1, NOTE_ROWS, width).astype(jnp.float32)
    strips = -(-rows // width)
    occ_all = (said[:, 0] + said[:, 1] + said[:, 2])[:, : pairs * strips].reshape(dests * pairs, strips * width)[:, :rows]
    occ_cols = jnp.transpose(jnp.pad(occ_all, ((0, width - dests * pairs), (0, 0))))
    notes = said[:, PARTS, 0].astype(jnp.int32)
    over = jnp.max(notes[:, slots * FIELDS]) > 0

    def finish(first, last, more, results):
        have = [code for part in codes[: last + 1] for code in part]
        inputs = (notes, occ_cols, vir_energy, amps_came, *have, *more, *results)
        counts = tuple(len(part) for part in codes[: last + 1])
        many = dests * slots
        return call(
            functools.partial(final_kernel, size, counts, bool(more), first, last, buffers),
            "update_tiles",
            inputs,
            [SMEM] + [VMEM] * 2 + [HBM] * (len(inputs) - 3),
            [jax.ShapeDtypeStruct((tiles, 1, *plain), jnp.float32)] * 2,
            [HBM] * 2,
            [counters(many)] * 5
            + [
                pltpu.VMEM((many, *coded), jnp.int16),
                pltpu.VMEM((many, *coded), jnp.int16),
                pltpu.VMEM((many, *plain), amps.dtype),
                pltpu.VMEM((buffers, 2, *plain), jnp.float32),
                dma((many,)),
                dma((many,)),
                dma((buffers, 2)),
            ],
            60,
            {len(inputs) - 2: 0, len(inputs) - 1: 1} if results else None,
        )

    results = finish(0, 0, [], ())

    def with_extra(results):
        more = call(
            functools.partial(pack_kernel, size),
            "pack_extra",
            (extra, amps),
            [SMEM, HBM],
            [jax.ShapeDtypeStruct((size.extra, *plain), amps.dtype)] * dests,
            [HBM] * dests,
            [
                pltpu.VMEM((dests * size.extra, *plain), amps.dtype),
                dma((dests * size.extra,)),
                dma((dests * size.extra,)),
            ],
            60,
        )
        more = [more[0]] + [swap(more[s], "occ", s) for s in range(1, dests)]
        return tuple(finish(1, chunks - 1, more, results))

    def without_extra(results):
        return tuple(finish(1, chunks - 1, [], results))

    return lax.cond(over, with_extra, without_extra, tuple(results))


def solution(mesh):
    return jax.shard_map(
        body,
        mesh=mesh,
        in_specs=(
            P(("groups", "occ"), None, "vir", None),
            P(("groups", "occ"), "vir"),
            P(("groups", "vir"), None, None, None),
            P(("groups", "vir"), None),
            P(("groups", "vir"), None, None),
            P(("groups", "occ"), None, None),
            P(("groups", "occ"), None),
            P(("groups", "vir"), None),
            P(("groups", "occ"), "vir"),
            P(("groups", "occ"), "vir"),
        ),
        out_specs=(
            P(("groups", "occ"), "vir", None, None),
            P(("groups", "occ"), "vir", None, None),
        ),
        check_vma=False,
    )
```

```python
import collections
import functools

import jax
import jax.numpy as jnp
from jax import lax
from jax.experimental import pallas as pl
from jax.experimental.pallas import tpu as pltpu
from jax.sharding import PartitionSpec as P

CODE_ROWS = 16
LEVELS = 32700.0
MIB = 1024 * 1024
AMPS = 1024
FIELDS = 4
NOTE_ROWS = 16
PARTS = 3
HBM = pl.BlockSpec(memory_space=pltpu.HBM)
SMEM = pl.BlockSpec(memory_space=pltpu.SMEM)
VMEM = pl.BlockSpec(memory_space=pltpu.VMEM)
SIZE_NAMES = ("pairs", "rows", "blocks", "width", "dests", "runs", "tiles", "slots", "early", "extra")
SIZE_NAMES += ("starts", "entries")
Size = collections.namedtuple("Size", SIZE_NAMES)


def call(kernel, name, inputs, in_specs, out_shape, out_specs, scratch, vmem, aliases=None):
    return pl.pallas_call(
        kernel,
        out_shape=out_shape,
        in_specs=in_specs,
        out_specs=out_specs,
        scratch_shapes=scratch,
        input_output_aliases=aliases or {},
        compiler_params=pltpu.CompilerParams(vmem_limit_bytes=vmem * MIB),
        name=name,
    )(*inputs)


def chunk_of(size, slot):
    return sum((slot >= start).astype(jnp.int32) for start in size.starts[1:-1])


def scale_block(rows):
    return 80 if rows % 80 == 0 else rows


def encode(values, out):
    rows, width = values.shape
    block = scale_block(rows)
    cut = values.reshape(rows // block, block, width)
    top = jnp.max(jnp.abs(cut), axis=1, keepdims=True)
    step = jnp.clip(jnp.ceil(8.0 * jnp.log2(jnp.maximum(top, 1e-30))), -800.0, 800.0)
    whole = jnp.round(cut * (LEVELS * jnp.exp2(step * -0.125))).reshape(rows, width)
    out[:rows, :] = whole.astype(jnp.int32).astype(jnp.int16)
    steps = step.reshape(rows // block, width)
    steps = jnp.concatenate([steps, jnp.zeros((CODE_ROWS - rows // block, width), jnp.float32)], axis=0)
    out[rows:, :] = steps.astype(jnp.int32).astype(jnp.int16)


def decode(coded):
    rows, width = coded.shape[0] - CODE_ROWS, coded.shape[1]
    block = scale_block(rows)
    steps = coded[rows:, :].astype(jnp.int32).astype(jnp.float32)[: rows // block]
    scale = jnp.exp2(steps * 0.125) * (1.0 / LEVELS)
    whole = coded[:rows, :].astype(jnp.int32).astype(jnp.float32)
    return (whole.reshape(rows // block, block, width) * scale.reshape(rows // block, 1, width)).reshape(rows, width)


def plan_kernel(size, place_in, res_keep_in, amp_keep_in, int_keep_in, occ_energy, amps, *refs):
    late, spots, wanted, extra, mask_own, mask_send, packed = refs[:7]
    place, res_keep, amp_keep, int_keep, word_sem = refs[7:12]
    notes, early_at, res_count, amp_count, all_count, res_seen, stage, energies, note, come_sem, go_sem, note_sem = refs[12:]
    words_in = [
        pltpu.make_async_copy(source, target, word_sem.at[n])
        for n, (source, target) in enumerate(
            ((place_in, place), (res_keep_in, res_keep), (amp_keep_in, amp_keep), (int_keep_in, int_keep))
        )
    ]
    for copy in words_in:
        copy.start()
    me, core = lax.axis_index("occ"), lax.rem(lax.axis_index("vir"), 2)

    for s in range(size.dests):
        for ref in (res_count, amp_count, all_count, res_seen):
            ref[s] = 0
    for n in range(size.dests * size.extra):
        extra[n] = -1
    for n in range(size.dests * size.early):
        early_at[n] = -1

    def clear(n, carry):
        late[n] = -1
        spots[n] = 0
        for f in range(FIELDS):
            notes[n * FIELDS + f] = 0
        return carry

    lax.fori_loop(0, size.entries, clear, 0)
    for n in range(size.tiles):
        wanted[n] = -1
    for copy in words_in:
        copy.wait()

    res_seen[size.dests] = 0

    def entry(s, slot):
        at = s * size.starts[1] + slot
        for low, high in zip(size.starts[1:-1], size.starts[2:]):
            at = jnp.where(slot >= low, low * size.dests + s * (high - low) + slot - low, at)
        return at

    def aim(pair, column):
        where = place[pair, column]
        target = sum((where >= n * size.tiles).astype(jnp.int32) for n in range(1, size.dests))
        return target ^ me, where - target * size.tiles

    def residuals(pair, carry):
        for column in range(size.blocks):
            s, _ = aim(pair, column)

            @pl.when(res_keep[pair, column] != 0)
            def _(column=column, s=s):
                slot = res_count[s]
                res_count[s] = slot + 1
                late[entry(s, slot)] = pair * size.blocks + column

        return carry

    lax.fori_loop(0, size.pairs, residuals, 0)

    def amplitudes(pair, carry):
        for column in range(size.blocks):
            tile = pair * size.blocks + column
            s, owned = aim(pair, column)
            first = (s * size.slots + all_count[s]) * FIELDS
            all_count[s] = all_count[s] + 1
            notes[first] = owned + 1
            notes[first + 1] = tile
            notes[first + 2] = -1
            notes[first + 3] = -1

            @pl.when(res_keep[pair, column] != 0)
            def _(s=s, first=first):
                notes[first + 2] = res_seen[s]
                res_seen[s] = res_seen[s] + 1

            @pl.when(amp_keep[pair, column] != 0)
            def _(s=s, first=first, tile=tile):
                rank = amp_count[s]
                amp_count[s] = rank + 1
                slot = size.slots - 1 - (rank - size.early)

                @pl.when(rank < size.early)
                def _():
                    n = s * size.early + rank
                    early_at[n] = tile
                    notes[first + 3] = rank
                    pltpu.make_async_copy(amps.at[tile], stage.at[n], come_sem.at[n]).start()

                @pl.when((rank >= size.early) & (slot >= res_count[s]))
                def _():
                    late[entry(s, slot)] = tile + AMPS
                    notes[first + 3] = size.early + slot

                @pl.when((rank >= size.early) & (slot < res_count[s]))
                def _():
                    extra[s * size.extra + rank - size.early] = tile
                    notes[first + 3] = size.slots + rank
                    res_seen[size.dests] = 1

        return carry

    lax.fori_loop(0, size.pairs, amplitudes, 0)

    for s in range(size.dests):
        for slot in range(size.early):
            n = s * size.early + slot

            @pl.when(early_at[n] >= 0)
            def _(s=s, slot=slot, n=n):
                rows = pl.ds(slot * size.rows, size.rows)
                pltpu.make_async_copy(amps.at[0], stage.at[n], come_sem.at[n]).wait()
                pltpu.make_async_copy(stage.at[n], packed.at[me ^ s, rows], go_sem.at[n]).start()

    energies[...] = jnp.zeros((NOTE_ROWS, size.width), jnp.float32)
    strips = -(-size.rows // size.width)
    for pair in range(size.pairs):
        for strip in range(strips):
            low, high = strip * size.width, min(size.rows, (strip + 1) * size.width)
            energies[pair * strips + strip : pair * strips + strip + 1, : high - low] = occ_energy[pair : pair + 1, low:high]
    left = energies[...]
    lane = lax.broadcasted_iota(jnp.int32, (NOTE_ROWS, size.width), 1)
    parts = []
    for _ in range(PARTS):
        parts.append(left.astype(jnp.bfloat16))
        left = left - parts[-1].astype(jnp.float32)
    for s in range(size.dests):
        for n, part in enumerate(parts):
            note[s, n * NOTE_ROWS : (n + 1) * NOTE_ROWS] = part
        words = jnp.where(lane == size.slots * FIELDS, res_seen[size.dests], 0)
        for n in range(size.slots * FIELDS):
            words = jnp.where(lane == n, notes[s * size.slots * FIELDS + n], words)
        note[s, PARTS * NOTE_ROWS :] = words.astype(jnp.float32).astype(jnp.bfloat16)
        target = packed.at[me ^ s, pl.ds(size.early * size.rows, (PARTS + 1) * NOTE_ROWS)]
        pltpu.make_async_copy(note.at[s], target, note_sem.at[s]).start()

    def compact(n, count):
        what = late[n]
        kept = (what >= 0) & (what < AMPS)

        @pl.when(kept)
        def _():
            wanted[count] = what
            spots[n] = count

        return count + kept.astype(jnp.int32)

    lax.fori_loop(0, size.entries, compact, jnp.int32(0))

    for pair in range(size.pairs):
        mask = amp_keep[pair, 0]
        for block in range(1, size.blocks):
            mask = mask | (amp_keep[pair, block] << block)
        mask_own[pair] = mask
        mask_send[pair] = mask

    def integrals(run, carry):
        for column in range(size.blocks):
            for target, parity in ((mask_own, core), (mask_send, 1 - core)):
                at = (run * 2 + parity) * size.blocks + column
                mask = int_keep[0, at]
                for block in range(1, size.blocks):
                    mask = mask | (int_keep[block, at] << block)
                target[size.pairs + run * size.blocks + column] = mask
        return carry

    lax.fori_loop(0, size.runs, integrals, 0)

    for s in range(size.dests):
        for slot in range(size.early):
            n = s * size.early + slot

            @pl.when(early_at[n] >= 0)
            def _(s=s, slot=slot, n=n):
                pltpu.make_async_copy(stage.at[n], packed.at[0, pl.ds(0, size.rows)], go_sem.at[n]).wait()

        target = packed.at[0, pl.ds(0, (PARTS + 1) * NOTE_ROWS)]
        pltpu.make_async_copy(note.at[s], target, note_sem.at[s]).wait()


def integral_tile(ints, place, wide):
    for first in range(0, ints.shape[1], 8):

        @pl.when((place >= first) & (place < first + 8))
        def _(first=first):
            part = ints[:, first : first + 8, :].astype(jnp.float32)
            wide[...] = part.reshape(wide.shape)

    return wide[pl.ds(lax.rem(place, 8), ints.shape[0], stride=8), :].astype(ints.dtype)


def ladder(size, span, wanted, run, masks, sources, totals, work, more, last):
    active, amps, ints, wide, amp_sem, int_sem = work
    amp_copies, int_copies = [], []
    for part in range(2):
        amp_copies.append(pltpu.make_async_copy(sources[2 * part], amps.at[part], amp_sem.at[part]))
        amp_copies[-1].start()
        int_copies.append([])
        for block in range(size.blocks):
            source = sources[2 * part + 1].at[block]
            int_copies[-1].append(pltpu.make_async_copy(source, ints.at[part, block], int_sem.at[part, block]))
            int_copies[-1][-1].start()
    core = lax.rem(lax.axis_index("vir"), 2)

    def prepare(n, carry):
        tile = wanted[n]
        active[n] = 0

        @pl.when(tile >= 0)
        def _():
            pair, column = tile // size.blocks, lax.rem(tile, size.blocks)
            at = size.pairs + run * size.blocks + column
            both = (masks[0][pair] & masks[0][at]) | ((masks[1][pair] & masks[1][at]) << size.blocks)
            active[n] = both
            totals[n] = jnp.zeros((size.rows, size.width), jnp.float32)

        return carry

    lax.fori_loop(*span, prepare, 0)
    for part in range(2):
        amp_copies[part].wait()
        if part == 0 and more is not None:

            def add_more(n, carry):
                @pl.when(wanted[n] >= 0)
                def _():
                    more(wanted[n], totals.at[n], amps.at[0])

                return carry

            lax.fori_loop(*span, add_more, 0)
        for block in range(size.blocks):
            int_copies[part][block].wait()
            bit = 1 << (part * size.blocks + block)

            def add(n, carry, part=part, block=block, bit=bit):
                @pl.when((active[n] & bit) != 0)
                def _():
                    tile = wanted[n]
                    pair, column = tile // size.blocks, lax.rem(tile, size.blocks)
                    place = (run * 2 + core) * size.blocks + column
                    totals[n] += jnp.dot(
                        amps[part, pair * size.blocks + block],
                        integral_tile(ints.at[part, block], place, wide),
                        preferred_element_type=jnp.float32,
                    )

                return carry

            lax.fori_loop(*span, add, 0)

    def leave(n, carry):
        @pl.when(wanted[n] >= 0)
        def _():
            last(n, totals.at[n])

        return carry

    lax.fori_loop(*span, leave, 0)


def sums_kernel(size, pieces, step, wanted, mask_own, mask_other, amps_own, ints_own, amps_other, ints_other, *refs):
    outs, refs = refs[: len(pieces)], refs[len(pieces) :]
    totals, work, (stage, sem) = refs[0], refs[1:7], refs[7:]
    run = (lax.axis_index("vir") // 2) ^ step
    span = (pieces[0][0], pieces[-1][1])

    def send(n, total):
        encode(total[...], stage.at[n])
        for out, (low, high) in zip(outs, pieces):

            @pl.when((n >= low) & (n < high))
            def _(out=out, low=low):
                pltpu.make_async_copy(stage.at[n], out.at[n - low], sem.at[n]).start()

    sources = (amps_own, ints_own, amps_other, ints_other)
    ladder(size, span, wanted, run, (mask_own, mask_other), sources, totals, work, None, send)

    def finish(n, carry):
        @pl.when(wanted[n] >= 0)
        def _():
            pltpu.make_async_copy(stage.at[n], outs[0].at[0], sem.at[n]).wait()

        return carry

    lax.fori_loop(*span, finish, 0)


def own_kernel(
    size, span, wanted, mask_own, mask_other, amps_own, ints_own, amps_other, ints_other, fock_vir, fock_occ, out, *refs
):
    totals, work, sem = refs[0], refs[1:7], refs[7]
    run = lax.axis_index("vir") // 2

    def fock(tile, total, amps):
        pair, column = tile // size.blocks, lax.rem(tile, size.blocks)

        @pl.when(((mask_own[pair] >> column) & 1) != 0)
        def _():
            kept = amps[tile]
            total[...] += jnp.dot(kept, fock_vir[column], preferred_element_type=jnp.float32)
            total[...] -= jnp.dot(fock_occ[pair], kept, preferred_element_type=jnp.float32)

    def send(n, total):
        pltpu.make_async_copy(total, out.at[n - span[0]], sem.at[n]).start()

    sources = (amps_own, ints_own, amps_other, ints_other)
    ladder(size, span, wanted, run, (mask_own, mask_other), sources, totals, work, fock, send)

    def finish(n, carry):
        @pl.when(wanted[n] >= 0)
        def _():
            pltpu.make_async_copy(totals.at[n], out.at[0], sem.at[n]).wait()

        return carry

    lax.fori_loop(*span, finish, 0)


def join_kernel(size, chunk, pieces, own_spans, others, late, spots, amps, *refs):
    own, refs = refs[: len(own_spans)], refs[len(own_spans) :]
    came, refs = refs[: others * len(pieces)], refs[others * len(pieces) :]
    outs, refs = refs[:-8], refs[-8:]
    own_here, came_here, amps_here, stage, own_sem, came_sem, amps_sem, out_sem = refs
    per_dest = size.starts[chunk + 1] - size.starts[chunk]
    first, many = size.starts[chunk] * size.dests, per_dest * size.dests

    def fetch(n, carry):
        what, spot = late[first + n], spots[first + n]

        @pl.when((what >= 0) & (what < AMPS))
        def _():
            for part, (low, high) in zip(own, own_spans):

                @pl.when((spot >= low) & (spot < high))
                def _(part=part, low=low):
                    pltpu.make_async_copy(part.at[spot - low], own_here.at[n], own_sem.at[n]).start()

            for k in range(others):
                for piece, (low, high) in enumerate(pieces):

                    @pl.when((spot >= low) & (spot < high))
                    def _(k=k, piece=piece, low=low):
                        source = came[k * len(pieces) + piece]
                        pltpu.make_async_copy(source.at[spot - low], came_here.at[k, n], came_sem.at[k, n]).start()

        @pl.when(what >= AMPS)
        def _():
            pltpu.make_async_copy(amps.at[what - AMPS], amps_here.at[n], amps_sem.at[n]).start()

        return carry

    def send(n):
        if len(outs) == 1:
            target = outs[0].at[(n // per_dest) ^ lax.axis_index("occ"), lax.rem(n, per_dest)]
            pltpu.make_async_copy(stage.at[n], target, out_sem.at[n]).start()
            return
        for s in range(size.dests):

            @pl.when(n // per_dest == s)
            def _(s=s):
                slot = lax.rem(n, per_dest)
                pltpu.make_async_copy(stage.at[n], outs[s].at[slot], out_sem.at[n]).start()

    def make(n, carry):
        what = late[first + n]

        @pl.when((what >= 0) & (what < AMPS))
        def _():
            pltpu.make_async_copy(own[0].at[0], own_here.at[n], own_sem.at[n]).wait()
            total = own_here[n]
            for k in range(others):
                pltpu.make_async_copy(came[0].at[0], came_here.at[k, n], came_sem.at[k, n]).wait()
                total = total + decode(came_here[k, n])
            encode(total, stage.at[n])
            send(n)

        @pl.when(what >= AMPS)
        def _():
            pltpu.make_async_copy(amps.at[0], amps_here.at[n], amps_sem.at[n]).wait()
            encode(amps_here[n].astype(jnp.float32), stage.at[n])
            send(n)

        return carry

    def finish(n, carry):
        @pl.when(late[first + n] >= 0)
        def _():
            target = outs[0].at[0, 0] if len(outs) == 1 else outs[0].at[0]
            pltpu.make_async_copy(stage.at[n], target, out_sem.at[n]).wait()

        return carry

    lax.fori_loop(0, many, fetch, 0)
    lax.fori_loop(0, many, make, 0)
    lax.fori_loop(0, many, finish, 0)


def pack_kernel(size, table, amps, *refs):
    outs, (stage, come_sem, go_sem) = refs[: size.dests], refs[size.dests :]

    def each(act):
        for s in range(size.dests):
            for slot in range(size.extra):
                n = s * size.extra + slot

                @pl.when(table[n] >= 0)
                def _(s=s, slot=slot, n=n):
                    act(s, slot, n)

    def come(s, slot, n):
        return pltpu.make_async_copy(amps.at[jnp.maximum(table[n], 0)], stage.at[n], come_sem.at[n])

    def go(s, slot, n):
        return pltpu.make_async_copy(stage.at[n], outs[s].at[slot], go_sem.at[n])

    def turn(*at):
        come(*at).wait()
        go(*at).start()

    each(lambda *at: come(*at).start())
    each(turn)
    each(lambda *at: go(*at).wait())


def final_kernel(size, counts, with_extra, first, last, buffers, notes, occ_cols, vir_energy, amps, *refs):
    codes = []
    for count in counts:
        codes.append(refs[:count])
        refs = refs[count:]
    me = lax.axis_index("occ")
    one_code = codes[0][0].at[0] if counts[0] > 1 else codes[0][0].at[0, 0]
    one_amps = amps.at[0, pl.ds(0, size.rows)]
    more = refs[: size.dests] if with_extra else None
    out_res, out_upd, slot_of, col_of, row_of, kind_of, has_res, res_here, code_here, amps_here, made = refs[-14:-3]
    res_sem, amps_sem, go_sem = refs[-3:]
    rows, width = made.shape[2], made.shape[3]

    def fetch_code(s, slot, target, sem):
        for chunk, parts in enumerate(codes):

            @pl.when(chunk_of(size, slot) == chunk)
            def _(chunk=chunk, parts=parts):
                at = slot - size.starts[chunk]
                source = parts[-s].at[at] if len(parts) > 1 else parts[0].at[s ^ me, at]
                pltpu.make_async_copy(source, target, sem).start()

    for s in range(size.dests):

        def fetch(n, carry, s=s):
            at = s * size.slots + n
            source = s ^ me
            owned, tile, res_slot, amp_slot = (notes[source, n * FIELDS + f] for f in range(FIELDS))
            amp_late = amp_slot - size.early
            is_late = (amp_late >= 0) & (amp_late < size.slots)
            is_extra = amp_late >= size.slots
            is_early = (amp_slot >= 0) & (amp_slot < size.early)
            needs = jnp.maximum(
                jnp.where(res_slot >= 0, chunk_of(size, res_slot), 0),
                jnp.where(is_extra, len(size.starts) - 2, jnp.where(is_late, chunk_of(size, amp_late), 0)),
            )
            mine = (owned > 0) & (needs >= first) & (needs <= last)
            slot_of[at] = jnp.where(mine, owned - 1, -1)
            pair = tile // size.blocks
            col_of[at] = source * size.pairs + pair
            row_of[at] = tile - pair * size.blocks
            kind_of[at] = jnp.where(is_late, 2, jnp.where(amp_slot >= 0, 1, 0))
            has_res[at] = (res_slot >= 0).astype(jnp.int32)

            @pl.when(mine & (res_slot >= 0))
            def _():
                fetch_code(s, res_slot, res_here.at[at], res_sem.at[at])

            @pl.when(mine & is_early)
            def _():
                place = pl.ds(pl.multiple_of(amp_slot * size.rows, 16), size.rows)
                pltpu.make_async_copy(amps.at[source, place], amps_here.at[at], amps_sem.at[at]).start()

            @pl.when(mine & is_late)
            def _():
                fetch_code(s, amp_late, code_here.at[at], amps_sem.at[at])

            if with_extra:

                @pl.when(mine & is_extra)
                def _():
                    spare = more[s].at[amp_late - size.slots]
                    pltpu.make_async_copy(spare, amps_here.at[at], amps_sem.at[at]).start()

            return carry

        lax.fori_loop(0, size.slots, fetch, 0)

    def leave(slot, buffer):
        return (
            pltpu.make_async_copy(made.at[buffer, 0], out_res.at[slot, 0], go_sem.at[buffer, 0]),
            pltpu.make_async_copy(made.at[buffer, 1], out_upd.at[slot, 0], go_sem.at[buffer, 1]),
        )

    def step(at, count):
        slot = slot_of[at]
        mine = slot >= 0
        buffer = lax.rem(count, buffers)

        @pl.when(mine)
        def _():
            @pl.when(count >= buffers)
            def _():
                for copy in leave(0, buffer):
                    copy.wait()

            kind = kind_of[at]

            @pl.when(kind == 0)
            def _():
                made[buffer, 1] = jnp.zeros((rows, width), jnp.float32)

            @pl.when(kind == 1)
            def _():
                pltpu.make_async_copy(one_amps, amps_here.at[at], amps_sem.at[at]).wait()
                made[buffer, 1] = amps_here[at].astype(jnp.float32)

            @pl.when(kind == 2)
            def _():
                pltpu.make_async_copy(one_code, code_here.at[at], amps_sem.at[at]).wait()
                made[buffer, 1] = decode(code_here[at])

            @pl.when(has_res[at] == 0)
            def _():
                made[buffer, 0] = jnp.zeros((rows, width), jnp.float32)

            @pl.when(has_res[at] != 0)
            def _():
                pltpu.make_async_copy(one_code, res_here.at[at], res_sem.at[at]).wait()
                resid = decode(res_here[at])
                lane = lax.broadcasted_iota(jnp.int32, (rows, width), 1)
                occ = jnp.sum(jnp.where(lane == col_of[at], occ_cols[...], 0.0), axis=1, keepdims=True)
                vir = vir_energy[pl.ds(row_of[at], 1), :]
                made[buffer, 0] = resid
                made[buffer, 1] += resid / (vir - occ)

            for copy in leave(slot, buffer):
                copy.start()

        return count + mine.astype(jnp.int32)

    count = lax.fori_loop(0, size.dests * size.slots, step, jnp.int32(0))
    for buffer in range(buffers):

        @pl.when(buffer < count)
        def _(buffer=buffer):
            for copy in leave(0, buffer):
                copy.wait()


def body(
    amplitudes,
    amp_keep,
    integrals,
    int_keep,
    fock_vir,
    fock_occ,
    occ_energy,
    vir_energy,
    res_keep,
    res_place,
):
    pairs, rows, blocks, width = amplitudes.shape
    dests, virs = lax.axis_size("occ"), lax.axis_size("vir")
    runs = virs // 2
    tiles = pairs * blocks
    slots = max(2, (tiles + dests - 1) // dests)
    early = max(1, 2 * slots // 3)
    starts = (0, slots // 3, slots * 2 // 3, slots) if slots % 3 == 0 else (0, 1, slots)
    chunks = len(starts) - 1
    entries = slots * dests
    size = Size(
        pairs, rows, blocks, width, dests, runs, tiles, slots, early, slots - early, starts, entries
    )
    coded = (rows + CODE_ROWS, width)
    plain = (rows, width)

    def swap(array, axis, bit):
        return lax.ppermute(array, axis, [(i, i ^ bit) for i in range(lax.axis_size(axis))])

    def words(count):
        return jax.ShapeDtypeStruct((count,), jnp.int32)

    def counters(count):
        return pltpu.SMEM((count,), jnp.int32)

    dma = pltpu.SemaphoreType.DMA

    amps = jnp.transpose(amplitudes, (0, 2, 1, 3)).reshape(tiles, rows, width)
    amps_other = swap(amps, "vir", 1)
    ints_other = swap(integrals, "vir", 1)

    sent_rows = early * rows + (PARTS + 1) * NOTE_ROWS
    late, spots, wanted, extra, mask_own, mask_send, packed = call(
        functools.partial(plan_kernel, size),
        "plan_tiles",
        (res_place, res_keep, amp_keep, int_keep, occ_energy, amps),
        [HBM] * 4 + [VMEM, HBM],
        [
            words(size.entries),
            words(size.entries),
            words(tiles),
            words(dests * size.extra),
            words(pairs + runs * blocks),
            words(pairs + runs * blocks),
            jax.ShapeDtypeStruct((dests, sent_rows, width), amps.dtype),
        ],
        [SMEM] * 6 + [HBM],
        [pltpu.SMEM(a.shape, jnp.int32) for a in (res_place, res_keep, amp_keep, int_keep)]
        + [dma((4,)), counters(dests * slots * FIELDS), counters(dests * early)]
        + [counters(dests)] * 3
        + [
            counters(dests + 1),
            pltpu.VMEM((dests * early, *plain), amps.dtype),
            pltpu.VMEM((NOTE_ROWS, width), jnp.float32),
            pltpu.VMEM((dests, (PARTS + 1) * NOTE_ROWS, width), amps.dtype),
            dma((dests * early,)),
            dma((dests * early,)),
            dma((dests,)),
        ],
        55,
    )
    wanted_other = [swap(wanted, "vir", 2 * k) for k in range(1, runs)]
    amps_came = lax.all_to_all(packed, "occ", split_axis=0, concat_axis=0, tiled=True)
    mask_other = swap(mask_send, "vir", 1)

    shared = (mask_own, mask_other, amps, integrals, amps_other, ints_other)
    share_specs = [SMEM] * 2 + [HBM] * 4
    work = [
        pltpu.VMEM((tiles, *plain), jnp.float32),
        counters(tiles),
        pltpu.VMEM((2, *amps.shape), amps.dtype),
        pltpu.VMEM((2, *integrals.shape), integrals.dtype),
        pltpu.VMEM((8 * width, width), jnp.float32),
        dma((2,)),
        dma((2, blocks)),
    ]

    bounds = [min(tiles, start * dests) for start in starts[1:-1]]
    bounds = sorted({0, *bounds, max(bounds[-1], tiles - tiles // 6), tiles})
    pieces = list(zip(bounds[:-1], bounds[1:]))
    rare = pieces[-1][0] >= tiles - tiles // 6 and len(pieces) > 1
    sums_came = []
    for k in range(1, runs):
        sums = []
        for some in (pieces[:1], pieces[1:]):
            if some:
                sums += call(
                    functools.partial(sums_kernel, size, some, k),
                    "ladder_sums",
                    (wanted_other[k - 1], *shared),
                    [SMEM] + share_specs,
                    [jax.ShapeDtypeStruct((high - low, *coded), jnp.int16) for low, high in some],
                    [HBM] * len(some),
                    [*work, pltpu.VMEM((tiles, *coded), jnp.int16), dma((tiles,))],
                    55,
                )
        came = [swap(part, "vir", 2 * k) for part in (sums[:-1] if rare else sums)]
        if rare:
            came.append(sums[-1])
        sums_came.append(came)

    def own_part(span, wanted):
        return call(
            functools.partial(own_kernel, size, span),
            "own_part",
            (wanted, *shared, fock_vir, fock_occ),
            [SMEM] + share_specs + [VMEM] * 2,
            jax.ShapeDtypeStruct((span[1] - span[0], *plain), jnp.float32),
            HBM,
            [*work, dma((tiles,))],
            55,
        )

    buffers = 4
    own_spans = [pieces[0]] + ([(pieces[0][1], tiles)] if len(pieces) > 1 else [])
    own = [own_part(own_spans[0], wanted)]

    codes = []
    for c in range(chunks):
        use = pieces if c == chunks - 1 else pieces[: min(c + 1, len(pieces))]
        per_dest = starts[c + 1] - starts[c]
        per_chunk = per_dest * dests
        if rare and c == chunks - 1:
            for k in range(1, runs):
                part, mine, theirs, _ = lax.optimization_barrier((sums_came[k - 1][-1], wanted, wanted_other[k - 1], joined[0]))
                beyond = (mine[use[-1][0]] >= 0) | (theirs[use[-1][0]] >= 0)
                sums_came[k - 1][-1] = lax.cond(
                    beyond, functools.partial(swap, axis="vir", bit=2 * k), lambda part: part, part
                )
        came = [part for parts in sums_came for part in parts[: len(use)]]
        if codes:
            late, after, _ = lax.optimization_barrier((late, wanted, joined[0]))
            if len(own) < len(own_spans):
                own.append(own_part(own_spans[1], after))
        spread = True
        outs = dests if spread else 1
        joined = call(
            functools.partial(join_kernel, size, c, use, own_spans[: len(own)], runs - 1),
            "join_parts",
            (late, spots, amps, *own, *came),
            [SMEM] * 2 + [HBM] * (1 + len(own) + len(came)),
            [jax.ShapeDtypeStruct((per_dest, *coded) if spread else (dests, per_dest, *coded), jnp.int16)] * outs,
            [HBM] * outs,
            [
                pltpu.VMEM((per_chunk, *plain), jnp.float32),
                pltpu.VMEM((runs - 1, per_chunk, *coded), jnp.int16),
                pltpu.VMEM((per_chunk, *plain), amps.dtype),
                pltpu.VMEM((per_chunk, *coded), jnp.int16),
                dma((per_chunk,)),
                dma((runs - 1, per_chunk)),
                dma((per_chunk,)),
                dma((per_chunk,)),
            ],
            60,
        )
        if spread:
            codes.append([joined[0]] + [swap(joined[s], "occ", s) for s in range(dests - 1, 0, -1)])
        else:
            codes.append([lax.all_to_all(joined[0], "occ", split_axis=0, concat_axis=0, tiled=True)])

    amps_came, _ = lax.optimization_barrier((amps_came, codes[0][0]))
    said = amps_came[:, early * rows :].reshape(dests, PARTS + 1, NOTE_ROWS, width).astype(jnp.float32)
    strips = -(-rows // width)
    occ_all = (said[:, 0] + said[:, 1] + said[:, 2])[:, : pairs * strips].reshape(dests * pairs, strips * width)[:, :rows]
    occ_cols = jnp.transpose(jnp.pad(occ_all, ((0, width - dests * pairs), (0, 0))))
    notes = said[:, PARTS, 0].astype(jnp.int32)
    over = jnp.max(notes[:, slots * FIELDS]) > 0

    def finish(first, last, more, results):
        have = [code for part in codes[: last + 1] for code in part]
        inputs = (notes, occ_cols, vir_energy, amps_came, *have, *more, *results)
        counts = tuple(len(part) for part in codes[: last + 1])
        many = dests * slots
        return call(
            functools.partial(final_kernel, size, counts, bool(more), first, last, buffers),
            "update_tiles",
            inputs,
            [SMEM] + [VMEM] * 2 + [HBM] * (len(inputs) - 3),
            [jax.ShapeDtypeStruct((tiles, 1, *plain), jnp.float32)] * 2,
            [HBM] * 2,
            [counters(many)] * 5
            + [
                pltpu.VMEM((many, *coded), jnp.int16),
                pltpu.VMEM((many, *coded), jnp.int16),
                pltpu.VMEM((many, *plain), amps.dtype),
                pltpu.VMEM((buffers, 2, *plain), jnp.float32),
                dma((many,)),
                dma((many,)),
                dma((buffers, 2)),
            ],
            60,
            {len(inputs) - 2: 0, len(inputs) - 1: 1} if results else None,
        )

    results = finish(0, 0, [], ())

    def with_extra(results):
        more = call(
            functools.partial(pack_kernel, size),
            "pack_extra",
            (extra, amps),
            [SMEM, HBM],
            [jax.ShapeDtypeStruct((size.extra, *plain), amps.dtype)] * dests,
            [HBM] * dests,
            [
                pltpu.VMEM((dests * size.extra, *plain), amps.dtype),
                dma((dests * size.extra,)),
                dma((dests * size.extra,)),
            ],
            60,
        )
        more = [more[0]] + [swap(more[s], "occ", s) for s in range(1, dests)]
        return tuple(finish(1, chunks - 1, more, results))

    def without_extra(results):
        return tuple(finish(1, chunks - 1, [], results))

    return lax.cond(over, with_extra, without_extra, tuple(results))


def solution(mesh):
    return jax.shard_map(
        body,
        mesh=mesh,
        in_specs=(
            P(("groups", "occ"), None, "vir", None),
            P(("groups", "occ"), "vir"),
            P(("groups", "vir"), None, None, None),
            P(("groups", "vir"), None),
            P(("groups", "vir"), None, None),
            P(("groups", "occ"), None, None),
            P(("groups", "occ"), None),
            P(("groups", "vir"), None),
            P(("groups", "occ"), "vir"),
            P(("groups", "occ"), "vir"),
        ),
        out_specs=(
            P(("groups", "occ"), "vir", None, None),
            P(("groups", "occ"), "vir", None, None),
        ),
        check_vma=False,
    )
```

```python
import collections
import functools

import jax
import jax.numpy as jnp
from jax import lax
from jax.experimental import pallas as pl
from jax.experimental.pallas import tpu as pltpu
from jax.sharding import PartitionSpec as P

CODE_ROWS = 16
LEVELS = 32700.0
MIB = 1024 * 1024
AMPS = 1024
FIELDS = 4
NOTE_ROWS = 16
PARTS = 3
HBM = pl.BlockSpec(memory_space=pltpu.HBM)
SMEM = pl.BlockSpec(memory_space=pltpu.SMEM)
VMEM = pl.BlockSpec(memory_space=pltpu.VMEM)
SIZE_NAMES = ("pairs", "rows", "blocks", "width", "dests", "runs", "tiles", "slots", "early", "extra")
SIZE_NAMES += ("starts", "entries")
Size = collections.namedtuple("Size", SIZE_NAMES)


def call(kernel, name, inputs, in_specs, out_shape, out_specs, scratch, vmem, aliases=None):
    return pl.pallas_call(
        kernel,
        out_shape=out_shape,
        in_specs=in_specs,
        out_specs=out_specs,
        scratch_shapes=scratch,
        input_output_aliases=aliases or {},
        compiler_params=pltpu.CompilerParams(vmem_limit_bytes=vmem * MIB),
        name=name,
    )(*inputs)


def chunk_of(size, slot):
    return sum((slot >= start).astype(jnp.int32) for start in size.starts[1:-1])


def scale_block(rows):
    return 80 if rows % 80 == 0 else rows


def encode(values, out):
    rows, width = values.shape
    block = scale_block(rows)
    cut = values.reshape(rows // block, block, width)
    top = jnp.max(jnp.abs(cut), axis=1, keepdims=True)
    step = jnp.clip(jnp.ceil(8.0 * jnp.log2(jnp.maximum(top, 1e-30))), -800.0, 800.0)
    whole = jnp.round(cut * (LEVELS * jnp.exp2(step * -0.125))).reshape(rows, width)
    out[:rows, :] = whole.astype(jnp.int32).astype(jnp.int16)
    steps = step.reshape(rows // block, width)
    steps = jnp.concatenate([steps, jnp.zeros((CODE_ROWS - rows // block, width), jnp.float32)], axis=0)
    out[rows:, :] = steps.astype(jnp.int32).astype(jnp.int16)


def decode(coded):
    rows, width = coded.shape[0] - CODE_ROWS, coded.shape[1]
    block = scale_block(rows)
    steps = coded[rows:, :].astype(jnp.int32).astype(jnp.float32)[: rows // block]
    scale = jnp.exp2(steps * 0.125) * (1.0 / LEVELS)
    whole = coded[:rows, :].astype(jnp.int32).astype(jnp.float32)
    return (whole.reshape(rows // block, block, width) * scale.reshape(rows // block, 1, width)).reshape(rows, width)


def plan_kernel(size, place_in, res_keep_in, amp_keep_in, int_keep_in, occ_energy, amps, *refs):
    late, spots, wanted, extra, mask_own, mask_send, packed = refs[:7]
    place, res_keep, amp_keep, int_keep, word_sem = refs[7:12]
    notes, early_at, res_count, amp_count, all_count, res_seen, stage, energies, note, come_sem, go_sem, note_sem = refs[12:]
    words_in = [
        pltpu.make_async_copy(source, target, word_sem.at[n])
        for n, (source, target) in enumerate(
            ((place_in, place), (res_keep_in, res_keep), (amp_keep_in, amp_keep), (int_keep_in, int_keep))
        )
    ]
    for copy in words_in:
        copy.start()
    me, core = lax.axis_index("occ"), lax.rem(lax.axis_index("vir"), 2)

    for s in range(size.dests):
        for ref in (res_count, amp_count, all_count, res_seen):
            ref[s] = 0
    for n in range(size.dests * size.extra):
        extra[n] = -1
    for n in range(size.dests * size.early):
        early_at[n] = -1

    def clear(n, carry):
        late[n] = -1
        spots[n] = 0
        for f in range(FIELDS):
            notes[n * FIELDS + f] = 0
        return carry

    lax.fori_loop(0, size.entries, clear, 0)
    for n in range(size.tiles):
        wanted[n] = -1
    for copy in words_in:
        copy.wait()

    res_seen[size.dests] = 0

    def entry(s, slot):
        at = s * size.starts[1] + slot
        for low, high in zip(size.starts[1:-1], size.starts[2:]):
            at = jnp.where(slot >= low, low * size.dests + s * (high - low) + slot - low, at)
        return at

    def aim(pair, column):
        where = place[pair, column]
        target = sum((where >= n * size.tiles).astype(jnp.int32) for n in range(1, size.dests))
        return target ^ me, where - target * size.tiles

    def residuals(pair, carry):
        for column in range(size.blocks):
            s, _ = aim(pair, column)

            @pl.when(res_keep[pair, column] != 0)
            def _(column=column, s=s):
                slot = res_count[s]
                res_count[s] = slot + 1
                late[entry(s, slot)] = pair * size.blocks + column

        return carry

    lax.fori_loop(0, size.pairs, residuals, 0)

    def amplitudes(pair, carry):
        for column in range(size.blocks):
            tile = pair * size.blocks + column
            s, owned = aim(pair, column)
            first = (s * size.slots + all_count[s]) * FIELDS
            all_count[s] = all_count[s] + 1
            notes[first] = owned + 1
            notes[first + 1] = tile
            notes[first + 2] = -1
            notes[first + 3] = -1

            @pl.when(res_keep[pair, column] != 0)
            def _(s=s, first=first):
                notes[first + 2] = res_seen[s]
                res_seen[s] = res_seen[s] + 1

            @pl.when(amp_keep[pair, column] != 0)
            def _(s=s, first=first, tile=tile):
                rank = amp_count[s]
                amp_count[s] = rank + 1
                slot = size.slots - 1 - (rank - size.early)

                @pl.when(rank < size.early)
                def _():
                    n = s * size.early + rank
                    early_at[n] = tile
                    notes[first + 3] = rank
                    pltpu.make_async_copy(amps.at[tile], stage.at[n], come_sem.at[n]).start()

                @pl.when((rank >= size.early) & (slot >= res_count[s]))
                def _():
                    late[entry(s, slot)] = tile + AMPS
                    notes[first + 3] = size.early + slot

                @pl.when((rank >= size.early) & (slot < res_count[s]))
                def _():
                    extra[s * size.extra + rank - size.early] = tile
                    notes[first + 3] = size.slots + rank
                    res_seen[size.dests] = 1

        return carry

    lax.fori_loop(0, size.pairs, amplitudes, 0)

    for s in range(size.dests):
        for slot in range(size.early):
            n = s * size.early + slot

            @pl.when(early_at[n] >= 0)
            def _(s=s, slot=slot, n=n):
                rows = pl.ds(slot * size.rows, size.rows)
                pltpu.make_async_copy(amps.at[0], stage.at[n], come_sem.at[n]).wait()
                pltpu.make_async_copy(stage.at[n], packed.at[me ^ s, rows], go_sem.at[n]).start()

    energies[...] = jnp.zeros((NOTE_ROWS, size.width), jnp.float32)
    strips = -(-size.rows // size.width)
    for pair in range(size.pairs):
        for strip in range(strips):
            low, high = strip * size.width, min(size.rows, (strip + 1) * size.width)
            energies[pair * strips + strip : pair * strips + strip + 1, : high - low] = occ_energy[pair : pair + 1, low:high]
    left = energies[...]
    lane = lax.broadcasted_iota(jnp.int32, (NOTE_ROWS, size.width), 1)
    parts = []
    for _ in range(PARTS):
        parts.append(left.astype(jnp.bfloat16))
        left = left - parts[-1].astype(jnp.float32)
    for s in range(size.dests):
        for n, part in enumerate(parts):
            note[s, n * NOTE_ROWS : (n + 1) * NOTE_ROWS] = part
        words = jnp.where(lane == size.slots * FIELDS, res_seen[size.dests], 0)
        for n in range(size.slots * FIELDS):
            words = jnp.where(lane == n, notes[s * size.slots * FIELDS + n], words)
        note[s, PARTS * NOTE_ROWS :] = words.astype(jnp.float32).astype(jnp.bfloat16)
        target = packed.at[me ^ s, pl.ds(size.early * size.rows, (PARTS + 1) * NOTE_ROWS)]
        pltpu.make_async_copy(note.at[s], target, note_sem.at[s]).start()

    def compact(n, count):
        what = late[n]
        kept = (what >= 0) & (what < AMPS)

        @pl.when(kept)
        def _():
            wanted[count] = what
            spots[n] = count

        return count + kept.astype(jnp.int32)

    lax.fori_loop(0, size.entries, compact, jnp.int32(0))

    for pair in range(size.pairs):
        mask = amp_keep[pair, 0]
        for block in range(1, size.blocks):
            mask = mask | (amp_keep[pair, block] << block)
        mask_own[pair] = mask
        mask_send[pair] = mask

    def integrals(run, carry):
        for column in range(size.blocks):
            for target, parity in ((mask_own, core), (mask_send, 1 - core)):
                at = (run * 2 + parity) * size.blocks + column
                mask = int_keep[0, at]
                for block in range(1, size.blocks):
                    mask = mask | (int_keep[block, at] << block)
                target[size.pairs + run * size.blocks + column] = mask
        return carry

    lax.fori_loop(0, size.runs, integrals, 0)

    for s in range(size.dests):
        for slot in range(size.early):
            n = s * size.early + slot

            @pl.when(early_at[n] >= 0)
            def _(s=s, slot=slot, n=n):
                pltpu.make_async_copy(stage.at[n], packed.at[0, pl.ds(0, size.rows)], go_sem.at[n]).wait()

        target = packed.at[0, pl.ds(0, (PARTS + 1) * NOTE_ROWS)]
        pltpu.make_async_copy(note.at[s], target, note_sem.at[s]).wait()


def integral_tile(ints, place, wide):
    for first in range(0, ints.shape[1], 8):

        @pl.when((place >= first) & (place < first + 8))
        def _(first=first):
            part = ints[:, first : first + 8, :].astype(jnp.float32)
            wide[...] = part.reshape(wide.shape)

    return wide[pl.ds(lax.rem(place, 8), ints.shape[0], stride=8), :].astype(ints.dtype)


def ladder(size, span, wanted, run, masks, sources, totals, work, more, last):
    active, amps, ints, wide, amp_sem, int_sem = work
    amp_copies, int_copies = [], []
    for part in range(2):
        amp_copies.append(pltpu.make_async_copy(sources[2 * part], amps.at[part], amp_sem.at[part]))
        amp_copies[-1].start()
        int_copies.append([])
        for block in range(size.blocks):
            source = sources[2 * part + 1].at[block]
            int_copies[-1].append(pltpu.make_async_copy(source, ints.at[part, block], int_sem.at[part, block]))
            int_copies[-1][-1].start()
    core = lax.rem(lax.axis_index("vir"), 2)

    def prepare(n, carry):
        tile = wanted[n]
        active[n] = 0

        @pl.when(tile >= 0)
        def _():
            pair, column = tile // size.blocks, lax.rem(tile, size.blocks)
            at = size.pairs + run * size.blocks + column
            both = (masks[0][pair] & masks[0][at]) | ((masks[1][pair] & masks[1][at]) << size.blocks)
            active[n] = both
            totals[n] = jnp.zeros((size.rows, size.width), jnp.float32)

        return carry

    lax.fori_loop(*span, prepare, 0)
    for part in range(2):
        amp_copies[part].wait()
        if part == 0 and more is not None:

            def add_more(n, carry):
                @pl.when(wanted[n] >= 0)
                def _():
                    more(wanted[n], totals.at[n], amps.at[0])

                return carry

            lax.fori_loop(*span, add_more, 0)
        for block in range(size.blocks):
            int_copies[part][block].wait()
            bit = 1 << (part * size.blocks + block)

            def add(n, carry, part=part, block=block, bit=bit):
                @pl.when((active[n] & bit) != 0)
                def _():
                    tile = wanted[n]
                    pair, column = tile // size.blocks, lax.rem(tile, size.blocks)
                    place = (run * 2 + core) * size.blocks + column
                    totals[n] += jnp.dot(
                        amps[part, pair * size.blocks + block],
                        integral_tile(ints.at[part, block], place, wide),
                        preferred_element_type=jnp.float32,
                    )

                return carry

            lax.fori_loop(*span, add, 0)

    def leave(n, carry):
        @pl.when(wanted[n] >= 0)
        def _():
            last(n, totals.at[n])

        return carry

    lax.fori_loop(*span, leave, 0)


def sums_kernel(size, pieces, step, wanted, mask_own, mask_other, amps_own, ints_own, amps_other, ints_other, *refs):
    outs, refs = refs[: len(pieces)], refs[len(pieces) :]
    totals, work, (stage, sem) = refs[0], refs[1:7], refs[7:]
    run = (lax.axis_index("vir") // 2) ^ step
    span = (pieces[0][0], pieces[-1][1])

    def send(n, total):
        encode(total[...], stage.at[n])
        for out, (low, high) in zip(outs, pieces):

            @pl.when((n >= low) & (n < high))
            def _(out=out, low=low):
                pltpu.make_async_copy(stage.at[n], out.at[n - low], sem.at[n]).start()

    sources = (amps_own, ints_own, amps_other, ints_other)
    ladder(size, span, wanted, run, (mask_own, mask_other), sources, totals, work, None, send)

    def finish(n, carry):
        @pl.when(wanted[n] >= 0)
        def _():
            pltpu.make_async_copy(stage.at[n], outs[0].at[0], sem.at[n]).wait()

        return carry

    lax.fori_loop(*span, finish, 0)


def own_kernel(
    size, span, wanted, mask_own, mask_other, amps_own, ints_own, amps_other, ints_other, fock_vir, fock_occ, out, *refs
):
    totals, work, sem = refs[0], refs[1:7], refs[7]
    run = lax.axis_index("vir") // 2

    def fock(tile, total, amps):
        pair, column = tile // size.blocks, lax.rem(tile, size.blocks)

        @pl.when(((mask_own[pair] >> column) & 1) != 0)
        def _():
            kept = amps[tile]
            total[...] += jnp.dot(kept, fock_vir[column], preferred_element_type=jnp.float32)
            total[...] -= jnp.dot(fock_occ[pair], kept, preferred_element_type=jnp.float32)

    def send(n, total):
        pltpu.make_async_copy(total, out.at[n - span[0]], sem.at[n]).start()

    sources = (amps_own, ints_own, amps_other, ints_other)
    ladder(size, span, wanted, run, (mask_own, mask_other), sources, totals, work, fock, send)

    def finish(n, carry):
        @pl.when(wanted[n] >= 0)
        def _():
            pltpu.make_async_copy(totals.at[n], out.at[0], sem.at[n]).wait()

        return carry

    lax.fori_loop(*span, finish, 0)


def join_kernel(size, chunk, pieces, own_spans, others, late, spots, amps, *refs):
    own, refs = refs[: len(own_spans)], refs[len(own_spans) :]
    came, refs = refs[: others * len(pieces)], refs[others * len(pieces) :]
    outs, refs = refs[:-8], refs[-8:]
    own_here, came_here, amps_here, stage, own_sem, came_sem, amps_sem, out_sem = refs
    per_dest = size.starts[chunk + 1] - size.starts[chunk]
    first, many = size.starts[chunk] * size.dests, per_dest * size.dests

    def fetch(n, carry):
        what, spot = late[first + n], spots[first + n]

        @pl.when((what >= 0) & (what < AMPS))
        def _():
            for part, (low, high) in zip(own, own_spans):

                @pl.when((spot >= low) & (spot < high))
                def _(part=part, low=low):
                    pltpu.make_async_copy(part.at[spot - low], own_here.at[n], own_sem.at[n]).start()

            for k in range(others):
                for piece, (low, high) in enumerate(pieces):

                    @pl.when((spot >= low) & (spot < high))
                    def _(k=k, piece=piece, low=low):
                        source = came[k * len(pieces) + piece]
                        pltpu.make_async_copy(source.at[spot - low], came_here.at[k, n], came_sem.at[k, n]).start()

        @pl.when(what >= AMPS)
        def _():
            pltpu.make_async_copy(amps.at[what - AMPS], amps_here.at[n], amps_sem.at[n]).start()

        return carry

    def send(n):
        if len(outs) == 1:
            target = outs[0].at[(n // per_dest) ^ lax.axis_index("occ"), lax.rem(n, per_dest)]
            pltpu.make_async_copy(stage.at[n], target, out_sem.at[n]).start()
            return
        for s in range(size.dests):

            @pl.when(n // per_dest == s)
            def _(s=s):
                slot = lax.rem(n, per_dest)
                pltpu.make_async_copy(stage.at[n], outs[s].at[slot], out_sem.at[n]).start()

    def make(n, carry):
        what = late[first + n]

        @pl.when((what >= 0) & (what < AMPS))
        def _():
            pltpu.make_async_copy(own[0].at[0], own_here.at[n], own_sem.at[n]).wait()
            total = own_here[n]
            for k in range(others):
                pltpu.make_async_copy(came[0].at[0], came_here.at[k, n], came_sem.at[k, n]).wait()
                total = total + decode(came_here[k, n])
            encode(total, stage.at[n])
            send(n)

        @pl.when(what >= AMPS)
        def _():
            pltpu.make_async_copy(amps.at[0], amps_here.at[n], amps_sem.at[n]).wait()
            encode(amps_here[n].astype(jnp.float32), stage.at[n])
            send(n)

        return carry

    def finish(n, carry):
        @pl.when(late[first + n] >= 0)
        def _():
            target = outs[0].at[0, 0] if len(outs) == 1 else outs[0].at[0]
            pltpu.make_async_copy(stage.at[n], target, out_sem.at[n]).wait()

        return carry

    lax.fori_loop(0, many, fetch, 0)
    lax.fori_loop(0, many, make, 0)
    lax.fori_loop(0, many, finish, 0)


def pack_kernel(size, table, amps, *refs):
    outs, (stage, come_sem, go_sem) = refs[: size.dests], refs[size.dests :]

    def each(act):
        for s in range(size.dests):
            for slot in range(size.extra):
                n = s * size.extra + slot

                @pl.when(table[n] >= 0)
                def _(s=s, slot=slot, n=n):
                    act(s, slot, n)

    def come(s, slot, n):
        return pltpu.make_async_copy(amps.at[jnp.maximum(table[n], 0)], stage.at[n], come_sem.at[n])

    def go(s, slot, n):
        return pltpu.make_async_copy(stage.at[n], outs[s].at[slot], go_sem.at[n])

    def turn(*at):
        come(*at).wait()
        go(*at).start()

    each(lambda *at: come(*at).start())
    each(turn)
    each(lambda *at: go(*at).wait())


def final_kernel(size, counts, with_extra, first, last, buffers, notes, occ_cols, vir_energy, amps, *refs):
    codes = []
    for count in counts:
        codes.append(refs[:count])
        refs = refs[count:]
    me = lax.axis_index("occ")
    one_code = codes[0][0].at[0] if counts[0] > 1 else codes[0][0].at[0, 0]
    one_amps = amps.at[0, pl.ds(0, size.rows)]
    more = refs[: size.dests] if with_extra else None
    out_res, out_upd, slot_of, col_of, row_of, kind_of, has_res, res_here, code_here, amps_here, made = refs[-14:-3]
    res_sem, amps_sem, go_sem = refs[-3:]
    rows, width = made.shape[2], made.shape[3]

    def fetch_code(s, slot, target, sem):
        for chunk, parts in enumerate(codes):

            @pl.when(chunk_of(size, slot) == chunk)
            def _(chunk=chunk, parts=parts):
                at = slot - size.starts[chunk]
                source = parts[-s].at[at] if len(parts) > 1 else parts[0].at[s ^ me, at]
                pltpu.make_async_copy(source, target, sem).start()

    for s in range(size.dests):

        def fetch(n, carry, s=s):
            at = s * size.slots + n
            source = s ^ me
            owned, tile, res_slot, amp_slot = (notes[source, n * FIELDS + f] for f in range(FIELDS))
            amp_late = amp_slot - size.early
            is_late = (amp_late >= 0) & (amp_late < size.slots)
            is_extra = amp_late >= size.slots
            is_early = (amp_slot >= 0) & (amp_slot < size.early)
            needs = jnp.maximum(
                jnp.where(res_slot >= 0, chunk_of(size, res_slot), 0),
                jnp.where(is_extra, len(size.starts) - 2, jnp.where(is_late, chunk_of(size, amp_late), 0)),
            )
            mine = (owned > 0) & (needs >= first) & (needs <= last)
            slot_of[at] = jnp.where(mine, owned - 1, -1)
            pair = tile // size.blocks
            col_of[at] = source * size.pairs + pair
            row_of[at] = tile - pair * size.blocks
            kind_of[at] = jnp.where(is_late, 2, jnp.where(amp_slot >= 0, 1, 0))
            has_res[at] = (res_slot >= 0).astype(jnp.int32)

            @pl.when(mine & (res_slot >= 0))
            def _():
                fetch_code(s, res_slot, res_here.at[at], res_sem.at[at])

            @pl.when(mine & is_early)
            def _():
                place = pl.ds(pl.multiple_of(amp_slot * size.rows, 16), size.rows)
                pltpu.make_async_copy(amps.at[source, place], amps_here.at[at], amps_sem.at[at]).start()

            @pl.when(mine & is_late)
            def _():
                fetch_code(s, amp_late, code_here.at[at], amps_sem.at[at])

            if with_extra:

                @pl.when(mine & is_extra)
                def _():
                    spare = more[s].at[amp_late - size.slots]
                    pltpu.make_async_copy(spare, amps_here.at[at], amps_sem.at[at]).start()

            return carry

        lax.fori_loop(0, size.slots, fetch, 0)

    def leave(slot, buffer):
        return (
            pltpu.make_async_copy(made.at[buffer, 0], out_res.at[slot, 0], go_sem.at[buffer, 0]),
            pltpu.make_async_copy(made.at[buffer, 1], out_upd.at[slot, 0], go_sem.at[buffer, 1]),
        )

    def step(at, count):
        slot = slot_of[at]
        mine = slot >= 0
        buffer = lax.rem(count, buffers)

        @pl.when(mine)
        def _():
            @pl.when(count >= buffers)
            def _():
                for copy in leave(0, buffer):
                    copy.wait()

            kind = kind_of[at]

            @pl.when(kind == 0)
            def _():
                made[buffer, 1] = jnp.zeros((rows, width), jnp.float32)

            @pl.when(kind == 1)
            def _():
                pltpu.make_async_copy(one_amps, amps_here.at[at], amps_sem.at[at]).wait()
                made[buffer, 1] = amps_here[at].astype(jnp.float32)

            @pl.when(kind == 2)
            def _():
                pltpu.make_async_copy(one_code, code_here.at[at], amps_sem.at[at]).wait()
                made[buffer, 1] = decode(code_here[at])

            @pl.when(has_res[at] == 0)
            def _():
                made[buffer, 0] = jnp.zeros((rows, width), jnp.float32)

            @pl.when(has_res[at] != 0)
            def _():
                pltpu.make_async_copy(one_code, res_here.at[at], res_sem.at[at]).wait()
                resid = decode(res_here[at])
                lane = lax.broadcasted_iota(jnp.int32, (rows, width), 1)
                occ = jnp.sum(jnp.where(lane == col_of[at], occ_cols[...], 0.0), axis=1, keepdims=True)
                vir = vir_energy[pl.ds(row_of[at], 1), :]
                made[buffer, 0] = resid
                made[buffer, 1] += resid / (vir - occ)

            for copy in leave(slot, buffer):
                copy.start()

        return count + mine.astype(jnp.int32)

    count = lax.fori_loop(0, size.dests * size.slots, step, jnp.int32(0))
    for buffer in range(buffers):

        @pl.when(buffer < count)
        def _(buffer=buffer):
            for copy in leave(0, buffer):
                copy.wait()


def body(
    amplitudes,
    amp_keep,
    integrals,
    int_keep,
    fock_vir,
    fock_occ,
    occ_energy,
    vir_energy,
    res_keep,
    res_place,
):
    pairs, rows, blocks, width = amplitudes.shape
    dests, virs = lax.axis_size("occ"), lax.axis_size("vir")
    runs = virs // 2
    tiles = pairs * blocks
    slots = max(2, (tiles + dests - 1) // dests)
    early = max(1, 2 * slots // 3)
    starts = (0, slots // 3, slots * 2 // 3, slots) if slots % 3 == 0 else (0, 1, slots)
    chunks = len(starts) - 1
    entries = slots * dests
    size = Size(
        pairs, rows, blocks, width, dests, runs, tiles, slots, early, slots - early, starts, entries
    )
    coded = (rows + CODE_ROWS, width)
    plain = (rows, width)

    def swap(array, axis, bit):
        return lax.ppermute(array, axis, [(i, i ^ bit) for i in range(lax.axis_size(axis))])

    def words(count):
        return jax.ShapeDtypeStruct((count,), jnp.int32)

    def counters(count):
        return pltpu.SMEM((count,), jnp.int32)

    dma = pltpu.SemaphoreType.DMA

    amps = jnp.transpose(amplitudes, (0, 2, 1, 3)).reshape(tiles, rows, width)
    amps_other = swap(amps, "vir", 1)
    ints_other = swap(integrals, "vir", 1)

    sent_rows = early * rows + (PARTS + 1) * NOTE_ROWS
    late, spots, wanted, extra, mask_own, mask_send, packed = call(
        functools.partial(plan_kernel, size),
        "plan_tiles",
        (res_place, res_keep, amp_keep, int_keep, occ_energy, amps),
        [HBM] * 4 + [VMEM, HBM],
        [
            words(size.entries),
            words(size.entries),
            words(tiles),
            words(dests * size.extra),
            words(pairs + runs * blocks),
            words(pairs + runs * blocks),
            jax.ShapeDtypeStruct((dests, sent_rows, width), amps.dtype),
        ],
        [SMEM] * 6 + [HBM],
        [pltpu.SMEM(a.shape, jnp.int32) for a in (res_place, res_keep, amp_keep, int_keep)]
        + [dma((4,)), counters(dests * slots * FIELDS), counters(dests * early)]
        + [counters(dests)] * 3
        + [
            counters(dests + 1),
            pltpu.VMEM((dests * early, *plain), amps.dtype),
            pltpu.VMEM((NOTE_ROWS, width), jnp.float32),
            pltpu.VMEM((dests, (PARTS + 1) * NOTE_ROWS, width), amps.dtype),
            dma((dests * early,)),
            dma((dests * early,)),
            dma((dests,)),
        ],
        55,
    )
    wanted_other = [swap(wanted, "vir", 2 * k) for k in range(1, runs)]
    amps_came = lax.all_to_all(packed, "occ", split_axis=0, concat_axis=0, tiled=True)
    mask_other = swap(mask_send, "vir", 1)

    shared = (mask_own, mask_other, amps, integrals, amps_other, ints_other)
    share_specs = [SMEM] * 2 + [HBM] * 4
    work = [
        pltpu.VMEM((tiles, *plain), jnp.float32),
        counters(tiles),
        pltpu.VMEM((2, *amps.shape), amps.dtype),
        pltpu.VMEM((2, *integrals.shape), integrals.dtype),
        pltpu.VMEM((8 * width, width), jnp.float32),
        dma((2,)),
        dma((2, blocks)),
    ]

    bounds = [min(tiles, start * dests) for start in starts[1:-1]]
    bounds = sorted({0, *bounds, max(bounds[-1], tiles - tiles // 6), tiles})
    pieces = list(zip(bounds[:-1], bounds[1:]))
    rare = pieces[-1][0] >= tiles - tiles // 6 and len(pieces) > 1
    sums_came = []
    for k in range(1, runs):
        sums = []
        for some in (pieces[:1], pieces[1:]):
            if some:
                sums += call(
                    functools.partial(sums_kernel, size, some, k),
                    "ladder_sums",
                    (wanted_other[k - 1], *shared),
                    [SMEM] + share_specs,
                    [jax.ShapeDtypeStruct((high - low, *coded), jnp.int16) for low, high in some],
                    [HBM] * len(some),
                    [*work, pltpu.VMEM((tiles, *coded), jnp.int16), dma((tiles,))],
                    55,
                )
        came = [swap(part, "vir", 2 * k) for part in (sums[:-1] if rare else sums)]
        if rare:
            came.append(sums[-1])
        sums_came.append(came)

    def own_part(span, wanted):
        return call(
            functools.partial(own_kernel, size, span),
            "own_part",
            (wanted, *shared, fock_vir, fock_occ),
            [SMEM] + share_specs + [VMEM] * 2,
            jax.ShapeDtypeStruct((span[1] - span[0], *plain), jnp.float32),
            HBM,
            [*work, dma((tiles,))],
            55,
        )

    buffers = 4
    own_spans = [pieces[0]] + ([(pieces[0][1], tiles)] if len(pieces) > 1 else [])
    own = [own_part(own_spans[0], wanted)]

    beyond = []
    if rare:
        for theirs in wanted_other:
            mine, theirs, _ = lax.optimization_barrier((wanted, theirs, own[0]))
            beyond.append(jnp.max(jnp.maximum(mine, theirs)[pieces[-1][0] :]) >= 0)

    codes = []
    for c in range(chunks):
        use = pieces if c == chunks - 1 else pieces[: min(c + 1, len(pieces))]
        per_dest = starts[c + 1] - starts[c]
        per_chunk = per_dest * dests
        if rare and c == chunks - 1:
            for k in range(1, runs):
                part, _ = lax.optimization_barrier((sums_came[k - 1][-1], joined[0]))
                sums_came[k - 1][-1] = lax.cond(
                    beyond[k - 1], functools.partial(swap, axis="vir", bit=2 * k), lambda part: part, part
                )
        came = [part for parts in sums_came for part in parts[: len(use)]]
        if codes:
            late, after, _ = lax.optimization_barrier((late, wanted, joined[0]))
            if len(own) < len(own_spans):
                own.append(own_part(own_spans[1], after))
        spread = True
        outs = dests if spread else 1
        joined = call(
            functools.partial(join_kernel, size, c, use, own_spans[: len(own)], runs - 1),
            "join_parts",
            (late, spots, amps, *own, *came),
            [SMEM] * 2 + [HBM] * (1 + len(own) + len(came)),
            [jax.ShapeDtypeStruct((per_dest, *coded) if spread else (dests, per_dest, *coded), jnp.int16)] * outs,
            [HBM] * outs,
            [
                pltpu.VMEM((per_chunk, *plain), jnp.float32),
                pltpu.VMEM((runs - 1, per_chunk, *coded), jnp.int16),
                pltpu.VMEM((per_chunk, *plain), amps.dtype),
                pltpu.VMEM((per_chunk, *coded), jnp.int16),
                dma((per_chunk,)),
                dma((runs - 1, per_chunk)),
                dma((per_chunk,)),
                dma((per_chunk,)),
            ],
            60,
        )
        if spread:
            codes.append([joined[0]] + [swap(joined[s], "occ", s) for s in range(dests - 1, 0, -1)])
        else:
            codes.append([lax.all_to_all(joined[0], "occ", split_axis=0, concat_axis=0, tiled=True)])

    amps_came, _ = lax.optimization_barrier((amps_came, codes[0][0]))
    said = amps_came[:, early * rows :].reshape(dests, PARTS + 1, NOTE_ROWS, width).astype(jnp.float32)
    strips = -(-rows // width)
    occ_all = (said[:, 0] + said[:, 1] + said[:, 2])[:, : pairs * strips].reshape(dests * pairs, strips * width)[:, :rows]
    occ_cols = jnp.transpose(jnp.pad(occ_all, ((0, width - dests * pairs), (0, 0))))
    notes = said[:, PARTS, 0].astype(jnp.int32)
    over = jnp.max(notes[:, slots * FIELDS]) > 0

    def finish(first, last, more, results):
        have = [code for part in codes[: last + 1] for code in part]
        inputs = (notes, occ_cols, vir_energy, amps_came, *have, *more, *results)
        counts = tuple(len(part) for part in codes[: last + 1])
        many = dests * slots
        return call(
            functools.partial(final_kernel, size, counts, bool(more), first, last, buffers),
            "update_tiles",
            inputs,
            [SMEM] + [VMEM] * 2 + [HBM] * (len(inputs) - 3),
            [jax.ShapeDtypeStruct((tiles, 1, *plain), jnp.float32)] * 2,
            [HBM] * 2,
            [counters(many)] * 5
            + [
                pltpu.VMEM((many, *coded), jnp.int16),
                pltpu.VMEM((many, *coded), jnp.int16),
                pltpu.VMEM((many, *plain), amps.dtype),
                pltpu.VMEM((buffers, 2, *plain), jnp.float32),
                dma((many,)),
                dma((many,)),
                dma((buffers, 2)),
            ],
            60,
            {len(inputs) - 2: 0, len(inputs) - 1: 1} if results else None,
        )

    results = finish(0, 0, [], ())

    def with_extra(results):
        more = call(
            functools.partial(pack_kernel, size),
            "pack_extra",
            (extra, amps),
            [SMEM, HBM],
            [jax.ShapeDtypeStruct((size.extra, *plain), amps.dtype)] * dests,
            [HBM] * dests,
            [
                pltpu.VMEM((dests * size.extra, *plain), amps.dtype),
                dma((dests * size.extra,)),
                dma((dests * size.extra,)),
            ],
            60,
        )
        more = [more[0]] + [swap(more[s], "occ", s) for s in range(1, dests)]
        return tuple(finish(1, chunks - 1, more, results))

    def without_extra(results):
        return tuple(finish(1, chunks - 1, [], results))

    return lax.cond(over, with_extra, without_extra, tuple(results))


def solution(mesh):
    return jax.shard_map(
        body,
        mesh=mesh,
        in_specs=(
            P(("groups", "occ"), None, "vir", None),
            P(("groups", "occ"), "vir"),
            P(("groups", "vir"), None, None, None),
            P(("groups", "vir"), None),
            P(("groups", "vir"), None, None),
            P(("groups", "occ"), None, None),
            P(("groups", "occ"), None),
            P(("groups", "vir"), None),
            P(("groups", "occ"), "vir"),
            P(("groups", "occ"), "vir"),
        ),
        out_specs=(
            P(("groups", "occ"), "vir", None, None),
            P(("groups", "occ"), "vir", None, None),
        ),
        check_vma=False,
    )
```
